32 devices in a mesh: groups: 2 (over y), dp: 4 (over z), pipe: 2 (over x), sub: 2 (over core).
Axes of the slice: x: 2, y: 2, z: 4, core: 2. Of those that a mesh axis runs over, the one named last changes fastest.
Arguments:
- tokens: bfloat16 [2, 2048, 8192], P('pipe', ('groups', 'dp'), 'sub'), parts along dimension 1, may hold values from -6 to 6
- cotangent: bfloat16 [2, 2048, 2, 1024], P('pipe', ('groups', 'dp')), parts along dimension 1, may hold values from -0.125 to 0.125
- frozen_weight: bfloat16 [2, 2, 1024, 8192], P('pipe', None, None, ('sub', 'dp')), may hold values from -0.0625 to 0.0625
- adapter_down: float32 [2, 64, 4, 8192], P('pipe', 'dp', 'groups', 'sub'), parts along dimension 2, may hold values from -0.0625 to 0.0625
- down_first_moment: float32 [2, 64, 4, 8192], P('pipe', 'dp', 'groups', 'sub'), parts along dimension 2, may hold values from -3 to 3
- down_second_moment: float32 [2, 64, 4, 8192], P('pipe', 'dp', 'groups', 'sub'), parts along dimension 2, may hold values from 0.05 to 2
- adapter_up: float32 [2, 1024, 4, 64], P('pipe', 'dp', 'groups'), parts along dimension 2, may hold values from -0.1875 to 0.1875
- up_first_moment: float32 [2, 1024, 4, 64], P('pipe', 'dp', 'groups'), parts along dimension 2, may hold values from -3 to 3
- up_second_moment: float32 [2, 1024, 4, 64], P('pipe', 'dp', 'groups'), parts along dimension 2, may hold values from 0.05 to 2
Outputs:
- merged_weight: bfloat16 [2, 4, 1024, 8192], P('pipe', 'groups', None, ('sub', 'dp')), parts along dimension 1
- new_down: float32 [2, 64, 4, 8192], P('pipe', 'dp', 'groups', 'sub'), parts along dimension 2
- new_down_moment: float32 [2, 64, 4, 8192], P('pipe', 'dp', 'groups', 'sub'), parts along dimension 2
- new_down_square: float32 [2, 64, 4, 8192], P('pipe', 'dp', 'groups', 'sub'), parts along dimension 2
- refreshed_up: float32 [2, 1024, 4, 64], P('pipe', 'dp', 'groups'), parts along dimension 2
- new_up_moment: float32 [2, 1024, 4, 64], P('pipe', 'dp', 'groups'), parts along dimension 2
- new_up_square: float32 [2, 1024, 4, 64], P('pipe', 'dp', 'groups'), parts along dimension 2
The draws below stay inside these ranges and needn't reach their ends.
There are 2 independent parts, one for each index of `groups`. The reference program is written for one: setup_inputs(seed, part) draws one part's arguments, and reference() takes and returns one part's arrays. A program takes and returns all parts, laid end to end along the dimension named above; an argument that names none is the same for every part. Nothing has to cross between parts.
All inputs are finite; a program needn't handle non-finite values.
Results may differ from the reference program's by a relative error of at most 0.0044.
Values may be sent and summed in bfloat16 or wider, within the bound.
A program may use at most 64 MiB of HBM per device.

```python
import math
import jax
import jax.numpy as jnp
from jax import lax

MODEL_WIDTH = 8192
KEY_VALUE_OUT = 1024
ADAPTER_RANK = 64
ADAM_STEP = 100
WINDOW_LAYERS = 2
TOKENS = 1024


def with_spikes(result, rng, source, target, blocks, factor):
    owner, partner = [(jnp.arange(result.shape[dim]) // (result.shape[dim] // blocks)).reshape([-1 if axis == dim else 1 for axis in range(result.ndim)]) for dim in (source, target)]
    chosen = jax.random.permutation(rng, blocks)[partner]
    strong = (owner == chosen) | (owner == (partner + blocks // 2) % blocks)
    return jnp.where(strong, factor * result, result)


def block_scale(own_key, dims, shards, smallest, largest):
    def one(dim, blocks):
        heights = jax.random.uniform(jax.random.fold_in(jax.random.fold_in(own_key, 6), dim), (blocks,), jnp.float32, smallest / len(shards), largest / len(shards))
        return jnp.repeat(jnp.exp(heights), dims[dim] // blocks).reshape((-1,) + (1,) * (len(dims) - dim - 1))

    gain = one(*shards[0])
    for cut in shards[1:]:
        gain = gain * one(*cut)
    return gain


def noise(rng, shape, scale, limit, pieces=(), kind=jnp.bfloat16):
    result = scale * jax.random.normal(rng, shape, jnp.float32)
    if pieces:
        result = result * block_scale(rng, shape, pieces, -0.22, 0.18)
    return jnp.clip(result, -limit, limit).astype(kind)


def bell_draw_with(rng, shape, width, reach, pieces, heavy, held_as=jnp.bfloat16):
    array = width * jax.random.normal(rng, shape, jnp.float32)
    if pieces:
        array = array * block_scale(rng, shape, pieces, -0.22, 0.18)
    return jnp.clip(with_spikes(array, jax.random.fold_in(rng, 3), *heavy), -reach, reach).astype(held_as)


def setup_inputs(seed: int = 0, part: int = 0) -> dict:
    splits = jax.random.split(jax.random.key(seed), 10)
    part_splits = jax.random.split(jax.random.fold_in(splits[9], part), 10)
    return {
        "tokens": noise(part_splits[0], (WINDOW_LAYERS, TOKENS, MODEL_WIDTH), 1.0, 6.0, ((0, 2), (1, 4), (2, 2))),
        "cotangent": bell_draw_with(part_splits[1], (WINDOW_LAYERS, TOKENS, 2, KEY_VALUE_OUT), (0.5 / TOKENS ** 0.5), 0.125, ((0, 2), (1, 4)), (1, 3, 4, 2.0)),
        "frozen_weight": noise(splits[2], (WINDOW_LAYERS, 2, KEY_VALUE_OUT, MODEL_WIDTH), MODEL_WIDTH ** -0.5, 0.0625, ((0, 2), (3, 8))),
        "adapter_down": noise(part_splits[3], (WINDOW_LAYERS, ADAPTER_RANK, 2, MODEL_WIDTH), MODEL_WIDTH ** -0.5, 0.0625, ((0, 2), (1, 4), (3, 2)), jnp.float32),
        "down_first_moment": noise(part_splits[4], (WINDOW_LAYERS, ADAPTER_RANK, 2, MODEL_WIDTH), 0.5, 3.0, ((0, 2), (1, 4), (3, 2)), jnp.float32),
        "down_second_moment": jnp.clip(jnp.exp(math.log(2.0) - 3.6888794 * jax.random.uniform(part_splits[5], (WINDOW_LAYERS, ADAPTER_RANK, 2, MODEL_WIDTH), jnp.float32) ** block_scale(part_splits[5], (WINDOW_LAYERS, ADAPTER_RANK, 2, MODEL_WIDTH), ((0, 2), (1, 4), (3, 2)), -0.2, 0.2)), 0.05, 2.0),
        "adapter_up": noise(part_splits[6], (WINDOW_LAYERS, KEY_VALUE_OUT, 2, ADAPTER_RANK), KEY_VALUE_OUT ** -0.5, 0.1875, ((0, 2), (1, 4)), jnp.float32),
        "up_first_moment": noise(part_splits[7], (WINDOW_LAYERS, KEY_VALUE_OUT, 2, ADAPTER_RANK), 0.5, 3.0, ((0, 2), (1, 4)), jnp.float32),
        "up_second_moment": jnp.clip(jnp.exp(math.log(2.0) - 3.6888794 * jax.random.uniform(part_splits[8], (WINDOW_LAYERS, KEY_VALUE_OUT, 2, ADAPTER_RANK), jnp.float32) ** block_scale(part_splits[8], (WINDOW_LAYERS, KEY_VALUE_OUT, 2, ADAPTER_RANK), ((0, 2), (1, 4)), -0.2, 0.2)), 0.05, 2.0),
    }


adapter_scale = 2.0
beta_one = 0.9
beta_two = 0.999
learn_rate = 0.005
adam_eps = 1e-08

def apply_adam_rule(current, moment, square, gradient):
    moment_new = beta_one * moment + (1.0 - beta_one) * gradient
    square_new = beta_two * square + (1.0 - beta_two) * gradient * gradient
    fix_first = 1.0 - beta_one ** ADAM_STEP
    fix_second = 1.0 - beta_two ** ADAM_STEP
    updated = current - learn_rate * (moment_new / fix_first) / (jnp.sqrt(square_new / fix_second) + adam_eps)
    return (updated, moment_new, square_new)

def rounded(values):
    return lax.optimization_barrier(values.astype(jnp.bfloat16)).astype(jnp.float32)

def single_layer_step(items):
    inputs, upstream, layer_start, down_now, down_first, down_sq, up_now, up_first_estimate, up_sq = items
    exact_precision = lax.Precision.HIGHEST
    input_gathered = inputs.astype(jnp.float32)
    upstream_gathered = upstream.astype(jnp.float32)
    down_used = rounded(down_now)
    up_used = rounded(up_now)
    rank_product = rounded(jnp.einsum('td,rmd->tmr', input_gathered, down_used, precision=exact_precision))
    reverse_pass = rounded(jnp.einsum('tmo,omr->tmr', upstream_gathered, up_used, precision=exact_precision))
    down_gradient = adapter_scale * jnp.einsum('qpj,qg->jpg', reverse_pass, input_gathered, precision=exact_precision)
    up_gradient = adapter_scale * jnp.einsum('iyq,iyv->qyv', upstream_gathered, rank_product, precision=exact_precision)
    new_down, new_down_moment, new_down_square = apply_adam_rule(down_now, down_first, down_sq, down_gradient)
    refreshed_up, new_up_moment, new_up_square = apply_adam_rule(up_now, up_first_estimate, up_sq, up_gradient)
    down_cast = rounded(new_down)
    up_cast = rounded(refreshed_up)
    weight_change = jnp.einsum('omr,rmd->mod', up_cast, down_cast, precision=exact_precision)
    combined_weight = (layer_start.astype(jnp.float32) + adapter_scale * weight_change).astype(jnp.bfloat16)
    return (combined_weight, new_down, new_down_moment, new_down_square, refreshed_up, new_up_moment, new_up_square)

def reference(tokens, cotangent, frozen_weight, adapter_down, down_first_moment, down_second_moment, adapter_up, up_first_moment, up_second_moment):
    layer_outputs = lax.map(single_layer_step, (tokens, cotangent, frozen_weight, adapter_down, down_first_moment, down_second_moment, adapter_up, up_first_moment, up_second_moment))
    return (layer_outputs[0], layer_outputs[1], layer_outputs[2], layer_outputs[3], layer_outputs[4], layer_outputs[5], layer_outputs[6])
```

```python
import functools

import jax
import jax.numpy as jnp
from jax import lax
from jax.experimental import pallas as pl
from jax.experimental.pallas import tpu as pltpu
from jax.sharding import PartitionSpec as P

ADAM_STEP = 100

adapter_scale = 2.0
beta_one = 0.9
beta_two = 0.999
learn_rate = 0.005
adam_eps = 1e-08

MESH = pl.DeviceIdType.MESH
UP, UP_CROSS, DOWN, GRAD_DOWN, LOW, GRAD_UP, NEW_UP, NEW_UP_CROSS, STATE, COLUMNS = range(10)
KINDS = 10


def apply_adam_rule(current, moment, square, gradient):
    moment_new = beta_one * moment + (1.0 - beta_one) * gradient
    square_new = beta_two * square + (1.0 - beta_two) * gradient * gradient
    fix_first = 1.0 - beta_one**ADAM_STEP
    fix_second = 1.0 - beta_two**ADAM_STEP
    updated = current - learn_rate * (moment_new / fix_first) / (
        jnp.sqrt(square_new / fix_second) + adam_eps
    )
    return (updated, moment_new, square_new)


def exchange_kernel(
    n,
    tok_hbm, cot_hbm, down, first_hbm, second_hbm, up, up_first, up_second,
    new_down, new_first, new_second, new_up, new_up_first, new_up_second, columns_out, up_out,
    tok, cot_raw, cot, first, second,
    up_all, down_all, back, grad_send, grad_recv, grad_own,
    low_own, low_send, low_recv, gu_send, gu_recv, gu_own, up_new_all, state, col_send, col_all,
    sems, local_sems,
):
    bf16, f32 = jnp.bfloat16, jnp.float32
    me = lax.axis_index("dp")
    core = lax.axis_index("sub")
    other = 1 - core
    rows = down.shape[0]
    rank = up.shape[1]
    kv_rows = up.shape[2]
    width = down.shape[2] // n

    def ahead(k):
        return lax.rem(me + k, n)

    def behind(k):
        return lax.rem(me + n - k, n)

    def to_learner(kind, k, src, dst):
        return pltpu.make_async_remote_copy(
            src_ref=src, dst_ref=dst,
            send_sem=sems.at[kind, 0, k], recv_sem=sems.at[kind, 1, k],
            device_id={"dp": ahead(k)}, device_id_type=MESH,
        )

    def to_core(kind, k, src, dst):
        return pltpu.make_async_remote_copy(
            src_ref=src, dst_ref=dst,
            send_sem=sems.at[kind, 0, k], recv_sem=sems.at[kind, 1, k],
            device_id={"sub": other}, device_id_type=MESH,
        )

    def loop(lo, hi, body):
        if n <= 4:
            for k in range(lo, hi):
                body(k)
        else:
            lax.fori_loop(lo, hi, lambda k, c: (body(k), c)[1], 0)

    locals_ = [
        pltpu.make_async_copy(src, dst, local_sems.at[i])
        for i, (src, dst) in enumerate(
            ((cot_hbm, cot_raw), (tok_hbm, tok), (first_hbm, first), (second_hbm, second))
        )
    ]
    for c in locals_:
        c.start()

    barrier = pltpu.get_barrier_semaphore()
    loop(1, n, lambda k: pl.semaphore_signal(
        barrier, inc=1, device_id={"dp": ahead(k)}, device_id_type=MESH))
    pl.semaphore_signal(barrier, inc=1, device_id={"sub": other}, device_id_type=MESH)

    up_all[me] = up[...].astype(bf16)
    for m in range(2):
        down_all[me, m] = down[:, m, :].astype(bf16)

    pl.semaphore_wait(barrier, n)

    def send_up(k):
        block = up_all.at[me, core]
        to_learner(UP, k, block, block).start()

    def send_down(k):
        block = down_all.at[me]
        to_learner(DOWN, k, block, block).start()

    loop(1, n, send_up)
    loop(1, n, send_down)

    locals_[0].wait()
    for m in range(2):
        cot[m] = cot_raw[:, m, :]

    def pass_up(k):
        block = up_all.at[behind(k), core]
        to_learner(UP, k, block, block).wait_recv()
        to_core(UP_CROSS, k, block, block).start()

    loop(1, n, pass_up)

    def got_up(k):
        block = up_all.at[behind(k), other]
        to_core(UP_CROSS, k, block, block).wait_recv()

    loop(1, n, got_up)

    for m in range(2):
        total = jnp.zeros((rank, tok.shape[0]), f32)
        for q in range(n):
            total = total + lax.dot_general(
                up_all[q, m], cot[m, :, q * kv_rows:(q + 1) * kv_rows],
                (((1,), (1,)), ((), ())), preferred_element_type=f32)
        total = total.astype(bf16)
        for q in range(n):
            back[q, m] = total[q * rows:(q + 1) * rows]

    locals_[1].wait()

    def grad_for(q):
        lhs = back[q].reshape(2 * rows, tok.shape[0])
        return adapter_scale * jnp.dot(lhs, tok[...], preferred_element_type=f32)

    def send_grad(k):
        q = ahead(k)
        g = grad_for(q).astype(bf16)
        grad_send[k, 0] = g[:rows]
        grad_send[k, 1] = g[rows:]
        to_learner(GRAD_DOWN, k, grad_send.at[k], grad_recv.at[k]).start()

    loop(1, n, send_grad)
    g = grad_for(me)
    grad_own[0] = g[:rows]
    grad_own[1] = g[rows:]

    def low_for(q):
        part = lax.dot_general(
            down_all[q].reshape(2 * rows, tok.shape[1]), tok[...],
            (((1,), (1,)), ((), ())), preferred_element_type=f32)
        for m in range(2):
            low_own[m, q] = part[m * rows:(m + 1) * rows]
            low_send[m, q] = part[m * rows:(m + 1) * rows].astype(bf16)

    low_for(me)

    def take_down(k):
        q = behind(k)
        block = down_all.at[q]
        to_learner(DOWN, k, block, block).wait_recv()
        low_for(q)

    loop(1, n, take_down)
    half = to_core(LOW, 0, low_send.at[other], low_recv)
    half.start()
    half.wait()
    lowrank = (low_own[core] + low_recv[...].astype(f32)).astype(bf16).reshape(rank, tok.shape[0])

    gu = adapter_scale * jnp.dot(lowrank, cot[core], preferred_element_type=f32)
    for q in range(n):
        gu_own[q] = gu[:, q * kv_rows:(q + 1) * kv_rows]
        gu_send[q] = gu[:, q * kv_rows:(q + 1) * kv_rows].astype(bf16)

    loop(1, n, lambda k: to_learner(GRAD_UP, k, gu_send.at[ahead(k)], gu_recv.at[k]).start())
    gu_own[n] = gu_own[me]

    def add_up(k):
        to_learner(GRAD_UP, k, gu_send.at[ahead(k)], gu_recv.at[k]).wait_recv()
        gu_own[n] = gu_own[n] + gu_recv[k].astype(f32)

    loop(1, n, add_up)
    p, f, s = apply_adam_rule(up[core], up_first[core], up_second[core], gu_own[n])
    up_new_all[me, core] = p.astype(bf16)

    def send_new_up(k):
        block = up_new_all.at[me, core]
        to_learner(NEW_UP, k, block, block).start()

    loop(1, n, send_new_up)
    state[core, 0] = p
    state[core, 1] = f
    state[core, 2] = s
    mine = to_core(STATE, 0, state.at[core], state.at[core])
    mine.start()

    locals_[2].wait()
    locals_[3].wait()
    loop(1, n, lambda k: to_learner(
        GRAD_DOWN, k, grad_send.at[k], grad_recv.at[k]).wait_recv())

    def adam_down(k):
        q = ahead(k)
        cols = pl.ds(pl.multiple_of(q * width, 128), width)
        for m in range(2):
            g = grad_own[m, :, cols]
            for j in range(1, n):
                g = g + grad_recv[j, m, :, cols].astype(f32)
            p, f, s = apply_adam_rule(down[:, m, cols], first[:, m, cols], second[:, m, cols], g)
            new_down[:, m, cols] = p
            new_first[:, m, cols] = f
            new_second[:, m, cols] = s
            if isinstance(k, int) and k == 0:
                col_all[me, m] = p.astype(bf16)
            else:
                col_send[k, m] = p.astype(bf16)

    def send_columns(k):
        adam_down(k)
        to_learner(COLUMNS, k, col_send.at[k], col_all.at[me]).start()

    loop(1, n, send_columns)
    adam_down(0)

    def pass_new_up(k):
        block = up_new_all.at[behind(k), core]
        to_learner(NEW_UP, k, block, block).wait_recv()
        to_core(NEW_UP_CROSS, k, block, block).start()

    loop(1, n, pass_new_up)
    to_core(STATE, 0, state.at[other], state.at[other]).wait_recv()
    for m in range(2):
        new_up[m] = state[m, 0]
        new_up_first[m] = state[m, 1]
        new_up_second[m] = state[m, 2]
    up_new_all[me, other] = state[other, 0].astype(bf16)

    def got_new_up(k):
        block = up_new_all.at[behind(k), other]
        to_core(NEW_UP_CROSS, k, block, block).wait_recv()

    loop(1, n, got_new_up)
    for m in range(2):
        for q in range(n):
            up_out[m, :, q * kv_rows:(q + 1) * kv_rows] = up_new_all[q, m]

    def got_columns(k):
        to_learner(COLUMNS, k, col_send.at[k], col_all.at[behind(k)]).wait_recv()

    loop(1, n, got_columns)
    for m in range(2):
        for q in range(n):
            columns_out[m, q * rows:(q + 1) * rows, :] = col_all[q, m]

    def sent(k):
        block = up_all.at[me, core]
        to_learner(UP, k, block, block).wait_send()
        block = up_all.at[behind(k), core]
        to_core(UP_CROSS, k, block, block).wait_send()
        block = down_all.at[me]
        to_learner(DOWN, k, block, block).wait_send()
        to_learner(GRAD_DOWN, k, grad_send.at[k], grad_recv.at[k]).wait_send()
        to_learner(GRAD_UP, k, gu_send.at[ahead(k)], gu_recv.at[k]).wait_send()
        block = up_new_all.at[me, core]
        to_learner(NEW_UP, k, block, block).wait_send()
        block = up_new_all.at[behind(k), core]
        to_core(NEW_UP_CROSS, k, block, block).wait_send()
        to_learner(COLUMNS, k, col_send.at[k], col_all.at[me]).wait_send()

    loop(1, n, sent)
    mine.wait_send()


def merge_kernel(
    frozen, up, columns, d0, d1, d2, u0, u1, u2,
    merged, e0, e1, e2, v0, v1, v2, sems,
):
    step = pl.program_id(0) * pl.num_programs(1) + pl.program_id(1)
    last = pl.num_programs(0) * pl.num_programs(1) - 1
    pairs = ((d0, e0), (d1, e1), (d2, e2), (u0, v0), (u1, v1), (u2, v2))
    copies = [pltpu.make_async_copy(a, b, sems.at[i]) for i, (a, b) in enumerate(pairs)]

    @pl.when(step == 0)
    def _():
        for c in copies:
            c.start()

    change = lax.dot_general(
        up[0], columns[0], (((0,), (0,)), ((), ())), preferred_element_type=jnp.float32)
    merged[0] = (frozen[0].astype(jnp.float32) + adapter_scale * change).astype(merged.dtype)

    @pl.when(step == last)
    def _():
        for c in copies:
            c.wait()


def local(
    n,
    tokens,
    cotangent,
    frozen_weight,
    adapter_down,
    down_first_moment,
    down_second_moment,
    adapter_up,
    up_first_moment,
    up_second_moment,
):
    bf16, f32 = jnp.bfloat16, jnp.float32
    tok, cot, frozen = tokens[0], cotangent[0], frozen_weight[0]
    down, first, second = adapter_down[0], down_first_moment[0], down_second_moment[0]
    up, up_first, up_second = [
        jnp.transpose(a[0], (1, 2, 0)) for a in (adapter_up, up_first_moment, up_second_moment)
    ]
    t, d = tok.shape
    _, kinds, o = cot.shape
    r = down.shape[0]
    rank, c = up.shape[1:]
    w = d // n
    vmem = pl.BlockSpec(memory_space=pltpu.VMEM)
    anywhere = pl.BlockSpec(memory_space=pl.ANY)
    down_like = jax.ShapeDtypeStruct(down.shape, f32)
    up_like = jax.ShapeDtypeStruct(up.shape, f32)
    outs = pl.pallas_call(
        functools.partial(exchange_kernel, n),
        out_shape=(
            down_like, down_like, down_like, up_like, up_like, up_like,
            jax.ShapeDtypeStruct((2, rank, w), bf16),
            jax.ShapeDtypeStruct((2, rank, o), bf16),
        ),
        in_specs=[anywhere, anywhere, vmem, anywhere, anywhere, vmem, vmem, vmem],
        out_specs=(vmem,) * 8,
        scratch_shapes=[
            pltpu.VMEM((t, d), bf16),
            pltpu.VMEM((t, 2, o), bf16),
            pltpu.VMEM((2, t, o), bf16),
            pltpu.VMEM((r, 2, d), f32),
            pltpu.VMEM((r, 2, d), f32),
            pltpu.VMEM((n, 2, rank, c), bf16),
            pltpu.VMEM((n, 2, r, d), bf16),
            pltpu.VMEM((n, 2, r, t), bf16),
            pltpu.VMEM((n, 2, r, d), bf16),
            pltpu.VMEM((n, 2, r, d), bf16),
            pltpu.VMEM((2, r, d), f32),
            pltpu.VMEM((2, n, r, t), f32),
            pltpu.VMEM((2, n, r, t), bf16),
            pltpu.VMEM((n, r, t), bf16),
            pltpu.VMEM((n, rank, c), bf16),
            pltpu.VMEM((n, rank, c), bf16),
            pltpu.VMEM((n + 1, rank, c), f32),
            pltpu.VMEM((n, 2, rank, c), bf16),
            pltpu.VMEM((2, 3, rank, c), f32),
            pltpu.VMEM((n, 2, r, w), bf16),
            pltpu.VMEM((n, 2, r, w), bf16),
            pltpu.SemaphoreType.DMA((KINDS, 2, n)),
            pltpu.SemaphoreType.DMA((4,)),
        ],
        compiler_params=pltpu.CompilerParams(
            collective_id=0, has_side_effects=True, vmem_limit_bytes=48 * 1024 * 1024
        ),
        cost_estimate=pl.CostEstimate(flops=10**9, bytes_accessed=10**7, transcendentals=0),
    )(tok, cot, down, first, second, up, up_first, up_second)
    columns, up_cast = outs[6], outs[7]
    block = min(256, o)
    merged, *rest = pl.pallas_call(
        merge_kernel,
        grid=(2, o // block),
        out_shape=(
            jax.ShapeDtypeStruct((2, o, w), bf16),
            down_like, down_like, down_like, up_like, up_like, up_like,
        ),
        in_specs=[
            pl.BlockSpec((1, block, w), lambda m, i: (m, i, 0)),
            pl.BlockSpec((1, rank, block), lambda m, i: (m, 0, i)),
            pl.BlockSpec((1, rank, w), lambda m, i: (m, 0, 0)),
        ] + [anywhere] * 6,
        out_specs=(pl.BlockSpec((1, block, w), lambda m, i: (m, i, 0)),) + (anywhere,) * 6,
        scratch_shapes=[pltpu.SemaphoreType.DMA((6,))],
        compiler_params=pltpu.CompilerParams(vmem_limit_bytes=32 * 1024 * 1024),
    )(frozen, up_cast, columns, *outs[:6])
    return (
        merged[None],
        rest[0][None],
        rest[1][None],
        rest[2][None],
        jnp.transpose(rest[3], (2, 0, 1))[None],
        jnp.transpose(rest[4], (2, 0, 1))[None],
        jnp.transpose(rest[5], (2, 0, 1))[None],
    )


def solution(mesh):
    return jax.shard_map(
        functools.partial(local, mesh.shape["dp"]),
        mesh=mesh,
        in_specs=(
            P("pipe", ("groups", "dp"), "sub"),
            P("pipe", ("groups", "dp"), None, None),
            P("pipe", None, None, ("sub", "dp")),
            P("pipe", "dp", "groups", "sub"),
            P("pipe", "dp", "groups", "sub"),
            P("pipe", "dp", "groups", "sub"),
            P("pipe", "dp", "groups", None),
            P("pipe", "dp", "groups", None),
            P("pipe", "dp", "groups", None),
        ),
        out_specs=(
            P("pipe", "groups", None, ("sub", "dp")),
            P("pipe", "dp", "groups", "sub"),
            P("pipe", "dp", "groups", "sub"),
            P("pipe", "dp", "groups", "sub"),
            P("pipe", "dp", "groups", None),
            P("pipe", "dp", "groups", None),
            P("pipe", "dp", "groups", None),
        ),
        check_vma=False,
    )
```

```python
import functools

import jax
import jax.numpy as jnp
from jax import lax
from jax.experimental import pallas as pl
from jax.experimental.pallas import tpu as pltpu
from jax.sharding import PartitionSpec as P

ADAM_STEP = 100

adapter_scale = 2.0
beta_one = 0.9
beta_two = 0.999
learn_rate = 0.005
adam_eps = 1e-08

MESH = pl.DeviceIdType.MESH
UP, UP_CROSS, DOWN, GRAD_DOWN, LOW, GRAD_UP, NEW_UP, NEW_UP_CROSS, STATE, COLUMNS, RELAY = range(11)
KINDS = 11


def apply_adam_rule(current, moment, square, gradient):
    moment_new = beta_one * moment + (1.0 - beta_one) * gradient
    square_new = beta_two * square + (1.0 - beta_two) * gradient * gradient
    fix_first = 1.0 - beta_one**ADAM_STEP
    fix_second = 1.0 - beta_two**ADAM_STEP
    updated = current - learn_rate * (moment_new / fix_first) / (
        jnp.sqrt(square_new / fix_second) + adam_eps
    )
    return (updated, moment_new, square_new)


def exchange_kernel(
    n,
    tok_hbm, cot_hbm, down_hbm, first_hbm, second_hbm, up_hbm, up_first_hbm, up_second_hbm,
    new_down, new_first, new_second, new_up, new_up_first, new_up_second, columns_out, up_out,
    tok, cot_raw, cot, down, first, second, up, up_first, up_second,
    up_all, down_all, back, grad_send, grad_recv, grad_own,
    low_own, low_send, low_recv, gu_send, gu_recv, gu_own, up_new_all, state, col_send, col_all,
    grad_relay, sems, local_sems,
):
    bf16, f32 = jnp.bfloat16, jnp.float32
    me = lax.axis_index("dp")
    core = lax.axis_index("sub")
    other = 1 - core
    rows = down.shape[0]
    rank = up.shape[1]
    kv_rows = up.shape[2]
    width = down.shape[2] // n

    def ahead(k):
        return lax.rem(me + k, n)

    def behind(k):
        return lax.rem(me + n - k, n)

    def to_learner(kind, k, src, dst):
        return pltpu.make_async_remote_copy(
            src_ref=src, dst_ref=dst,
            send_sem=sems.at[kind, 0, k], recv_sem=sems.at[kind, 1, k],
            device_id={"dp": ahead(k)}, device_id_type=MESH,
        )

    def to_core(kind, k, src, dst):
        return pltpu.make_async_remote_copy(
            src_ref=src, dst_ref=dst,
            send_sem=sems.at[kind, 0, k], recv_sem=sems.at[kind, 1, k],
            device_id={"sub": other}, device_id_type=MESH,
        )

    relayed = n == 4
    if relayed:
        middle = jnp.logical_and(me > 0, me < 3)
        toward = jnp.where(me < 2, 3, 1)
        near = 4 - toward
        beside = lax.rem(3 * me + 1, 4)

    def loop(lo, hi, body):
        if n <= 4:
            for k in range(lo, hi):
                body(k)
        else:
            lax.fori_loop(lo, hi, lambda k, c: (body(k), c)[1], 0)

    locals_ = [
        pltpu.make_async_copy(src, dst, local_sems.at[i])
        for i, (src, dst) in enumerate(
            (
                (up_hbm, up), (down_hbm, down), (cot_hbm, cot_raw), (tok_hbm, tok),
                (up_first_hbm, up_first), (up_second_hbm, up_second),
                (first_hbm, first), (second_hbm, second),
            )
        )
    ]
    for c in locals_:
        c.start()

    barrier = pltpu.get_barrier_semaphore()
    loop(1, n, lambda k: pl.semaphore_signal(
        barrier, inc=1, device_id={"dp": ahead(k)}, device_id_type=MESH))
    pl.semaphore_signal(barrier, inc=1, device_id={"sub": other}, device_id_type=MESH)

    locals_[0].wait()
    up_all[me] = up[...].astype(bf16)
    locals_[1].wait()
    for m in range(2):
        down_all[me, m] = down[:, m, :].astype(bf16)

    pl.semaphore_wait(barrier, n)

    def send_up(k):
        block = up_all.at[me, core]
        to_learner(UP, k, block, block).start()

    def send_down(k):
        block = down_all.at[me]
        to_learner(DOWN, k, block, block).start()

    loop(1, n, send_up)
    if relayed:
        send_down(2)
        for k in (toward, near):
            pl.when(jnp.logical_or(middle, k != toward))(functools.partial(send_down, k))

        @pl.when(jnp.logical_not(middle))
        def _():
            grad_recv[near] = jnp.zeros(grad_recv.shape[1:], bf16)
    else:
        loop(1, n, send_down)

    locals_[2].wait()
    for m in range(2):
        cot[m] = cot_raw[:, m, :]

    def pass_up(k):
        block = up_all.at[behind(k), core]
        to_learner(UP, k, block, block).wait_recv()
        to_core(UP_CROSS, k, block, block).start()

    loop(1, n, pass_up)

    def got_up(k):
        block = up_all.at[behind(k), other]
        to_core(UP_CROSS, k, block, block).wait_recv()

    loop(1, n, got_up)

    for m in range(2):
        total = jnp.zeros((rank, tok.shape[0]), f32)
        for q in range(n):
            total = total + lax.dot_general(
                up_all[q, m], cot[m, :, q * kv_rows:(q + 1) * kv_rows],
                (((1,), (1,)), ((), ())), preferred_element_type=f32)
        total = total.astype(bf16)
        for q in range(n):
            back[q, m] = total[q * rows:(q + 1) * rows]

    locals_[3].wait()

    def grad_for(q):
        lhs = back[q].reshape(2 * rows, tok.shape[0])
        return adapter_scale * jnp.dot(lhs, tok[...], preferred_element_type=f32)

    def send_grad(k):
        q = ahead(k)
        g = grad_for(q).astype(bf16)
        grad_send[k, 0] = g[:rows]
        grad_send[k, 1] = g[rows:]
        to_learner(GRAD_DOWN, k, grad_send.at[k], grad_recv.at[k]).start()

    if relayed:
        relay_in = pltpu.make_async_remote_copy(
            src_ref=grad_send.at[0], dst_ref=grad_relay,
            send_sem=sems.at[RELAY, 0, 0], recv_sem=sems.at[RELAY, 1, 0],
            device_id={"dp": beside}, device_id_type=MESH,
        )

        @pl.when(middle)
        def _():
            send_grad(toward)
            send_grad(near)

        @pl.when(jnp.logical_not(middle))
        def _():
            g = grad_for(ahead(toward)).astype(bf16)
            grad_send[0, 0] = g[:rows]
            grad_send[0, 1] = g[rows:]
            relay_in.start()
            send_grad(2)
            send_grad(near)
    else:
        loop(1, n, send_grad)
    g = grad_for(me)
    grad_own[0] = g[:rows]
    grad_own[1] = g[rows:]

    def low_for(q):
        part = lax.dot_general(
            down_all[q].reshape(2 * rows, tok.shape[1]), tok[...],
            (((1,), (1,)), ((), ())), preferred_element_type=f32)
        for m in range(2):
            low_own[m, q] = part[m * rows:(m + 1) * rows]
            low_send[m, q] = part[m * rows:(m + 1) * rows].astype(bf16)

    low_for(me)

    def take_down(k):
        q = behind(k)
        block = down_all.at[q]
        to_learner(DOWN, k, block, block).wait_recv()
        low_for(q)

    down_relay = None
    if relayed:
        take_down(2)
        block = down_all.at[behind(2)]
        down_relay = pltpu.make_async_remote_copy(
            src_ref=block, dst_ref=block,
            send_sem=sems.at[RELAY, 0, 1], recv_sem=sems.at[DOWN, 1, lax.rem(2 * me + 3, 4)],
            device_id={"dp": beside}, device_id_type=MESH,
        )

        @pl.when(middle)
        def _():
            down_relay.start()
            g = grad_for(ahead(2))
            relay_in.wait_recv()
            for m in range(2):
                grad_send[2, m] = (
                    g[m * rows:(m + 1) * rows] + grad_relay[m].astype(f32)).astype(bf16)
            to_learner(GRAD_DOWN, 2, grad_send.at[2], grad_recv.at[2]).start()

        take_down(toward)
        take_down(near)
    else:
        loop(1, n, take_down)
    half = to_core(LOW, 0, low_send.at[other], low_recv)
    half.start()
    half.wait()
    lowrank = (low_own[core] + low_recv[...].astype(f32)).astype(bf16).reshape(rank, tok.shape[0])

    gu = adapter_scale * jnp.dot(lowrank, cot[core], preferred_element_type=f32)
    for q in range(n):
        gu_own[q] = gu[:, q * kv_rows:(q + 1) * kv_rows]
        gu_send[q] = gu[:, q * kv_rows:(q + 1) * kv_rows].astype(bf16)

    loop(1, n, lambda k: to_learner(GRAD_UP, k, gu_send.at[ahead(k)], gu_recv.at[k]).start())
    gu_own[n] = gu_own[me]

    def add_up(k):
        to_learner(GRAD_UP, k, gu_send.at[ahead(k)], gu_recv.at[k]).wait_recv()
        gu_own[n] = gu_own[n] + gu_recv[k].astype(f32)

    loop(1, n, add_up)
    locals_[4].wait()
    locals_[5].wait()
    p, f, s = apply_adam_rule(up[core], up_first[core], up_second[core], gu_own[n])
    up_new_all[me, core] = p.astype(bf16)

    def send_new_up(k):
        block = up_new_all.at[me, core]
        to_learner(NEW_UP, k, block, block).start()

    loop(1, n, send_new_up)
    state[core, 0] = p
    state[core, 1] = f
    state[core, 2] = s
    mine = to_core(STATE, 0, state.at[core], state.at[core])
    mine.start()

    locals_[6].wait()
    locals_[7].wait()

    def got_grad(k):
        to_learner(GRAD_DOWN, k, grad_send.at[k], grad_recv.at[k]).wait_recv()

    if relayed:
        got_grad(2)
        got_grad(toward)
        pl.when(middle)(functools.partial(got_grad, near))
    else:
        loop(1, n, got_grad)

    def adam_down(k):
        q = ahead(k)
        cols = pl.ds(pl.multiple_of(q * width, 128), width)
        for m in range(2):
            g = grad_own[m, :, cols]
            for j in range(1, n):
                g = g + grad_recv[j, m, :, cols].astype(f32)
            p, f, s = apply_adam_rule(down[:, m, cols], first[:, m, cols], second[:, m, cols], g)
            new_down[:, m, cols] = p
            new_first[:, m, cols] = f
            new_second[:, m, cols] = s
            if isinstance(k, int) and k == 0:
                col_all[me, m] = p.astype(bf16)
            else:
                col_send[k, m] = p.astype(bf16)

    def send_columns(k):
        adam_down(k)
        to_learner(COLUMNS, k, col_send.at[k], col_all.at[me]).start()

    loop(1, n, send_columns)
    adam_down(0)

    def pass_new_up(k):
        block = up_new_all.at[behind(k), core]
        to_learner(NEW_UP, k, block, block).wait_recv()
        to_core(NEW_UP_CROSS, k, block, block).start()

    loop(1, n, pass_new_up)
    to_core(STATE, 0, state.at[other], state.at[other]).wait_recv()
    for m in range(2):
        new_up[m] = state[m, 0]
        new_up_first[m] = state[m, 1]
        new_up_second[m] = state[m, 2]
    up_new_all[me, other] = state[other, 0].astype(bf16)

    def got_new_up(k):
        block = up_new_all.at[behind(k), other]
        to_core(NEW_UP_CROSS, k, block, block).wait_recv()

    loop(1, n, got_new_up)
    for m in range(2):
        for q in range(n):
            up_out[m, :, q * kv_rows:(q + 1) * kv_rows] = up_new_all[q, m]

    def got_columns(k):
        to_learner(COLUMNS, k, col_send.at[k], col_all.at[behind(k)]).wait_recv()

    loop(1, n, got_columns)
    for m in range(2):
        for q in range(n):
            columns_out[m, q * rows:(q + 1) * rows, :] = col_all[q, m]

    def sent(k):
        block = up_all.at[me, core]
        to_learner(UP, k, block, block).wait_send()
        block = up_all.at[behind(k), core]
        to_core(UP_CROSS, k, block, block).wait_send()
        to_learner(GRAD_UP, k, gu_send.at[ahead(k)], gu_recv.at[k]).wait_send()
        block = up_new_all.at[me, core]
        to_learner(NEW_UP, k, block, block).wait_send()
        block = up_new_all.at[behind(k), core]
        to_core(NEW_UP_CROSS, k, block, block).wait_send()
        to_learner(COLUMNS, k, col_send.at[k], col_all.at[me]).wait_send()

    def sent_down(k):
        block = down_all.at[me]
        to_learner(DOWN, k, block, block).wait_send()
        to_learner(GRAD_DOWN, k, grad_send.at[k], grad_recv.at[k]).wait_send()

    loop(1, n, sent)
    if relayed:
        sent_down(2)
        sent_down(near)

        @pl.when(middle)
        def _():
            sent_down(toward)
            down_relay.wait_send()

        @pl.when(jnp.logical_not(middle))
        def _():
            relay_in.wait_send()
    else:
        loop(1, n, sent_down)
    mine.wait_send()


def merge_kernel(
    frozen, up, columns, d0, d1, d2, u0, u1, u2,
    merged, e0, e1, e2, v0, v1, v2, sems,
):
    step = pl.program_id(0) * pl.num_programs(1) + pl.program_id(1)
    last = pl.num_programs(0) * pl.num_programs(1) - 1
    pairs = ((d0, e0), (d1, e1), (d2, e2), (u0, v0), (u1, v1), (u2, v2))
    copies = [pltpu.make_async_copy(a, b, sems.at[i]) for i, (a, b) in enumerate(pairs)]

    @pl.when(step == 0)
    def _():
        for c in copies:
            c.start()

    change = lax.dot_general(
        up[0], columns[0], (((0,), (0,)), ((), ())), preferred_element_type=jnp.float32)
    merged[0] = (frozen[0].astype(jnp.float32) + adapter_scale * change).astype(merged.dtype)

    @pl.when(step == last)
    def _():
        for c in copies:
            c.wait()


def local(
    n,
    tokens,
    cotangent,
    frozen_weight,
    adapter_down,
    down_first_moment,
    down_second_moment,
    adapter_up,
    up_first_moment,
    up_second_moment,
):
    bf16, f32 = jnp.bfloat16, jnp.float32
    tok, cot, frozen = tokens[0], cotangent[0], frozen_weight[0]
    down, first, second = adapter_down[0], down_first_moment[0], down_second_moment[0]
    up, up_first, up_second = [
        jnp.transpose(a[0], (1, 2, 0)) for a in (adapter_up, up_first_moment, up_second_moment)
    ]
    t, d = tok.shape
    _, kinds, o = cot.shape
    r = down.shape[0]
    rank, c = up.shape[1:]
    w = d // n
    vmem = pl.BlockSpec(memory_space=pltpu.VMEM)
    anywhere = pl.BlockSpec(memory_space=pl.ANY)
    down_like = jax.ShapeDtypeStruct(down.shape, f32)
    up_like = jax.ShapeDtypeStruct(up.shape, f32)
    outs = pl.pallas_call(
        functools.partial(exchange_kernel, n),
        out_shape=(
            down_like, down_like, down_like, up_like, up_like, up_like,
            jax.ShapeDtypeStruct((2, rank, w), bf16),
            jax.ShapeDtypeStruct((2, rank, o), bf16),
        ),
        in_specs=[pl.BlockSpec(memory_space=pltpu.HBM)] * 8,
        out_specs=(vmem,) * 8,
        scratch_shapes=[
            pltpu.VMEM((t, d), bf16),
            pltpu.VMEM((t, 2, o), bf16),
            pltpu.VMEM((2, t, o), bf16),
            pltpu.VMEM((r, 2, d), f32),
            pltpu.VMEM((r, 2, d), f32),
            pltpu.VMEM((r, 2, d), f32),
            pltpu.VMEM((2, rank, c), f32),
            pltpu.VMEM((2, rank, c), f32),
            pltpu.VMEM((2, rank, c), f32),
            pltpu.VMEM((n, 2, rank, c), bf16),
            pltpu.VMEM((n, 2, r, d), bf16),
            pltpu.VMEM((n, 2, r, t), bf16),
            pltpu.VMEM((n, 2, r, d), bf16),
            pltpu.VMEM((n, 2, r, d), bf16),
            pltpu.VMEM((2, r, d), f32),
            pltpu.VMEM((2, n, r, t), f32),
            pltpu.VMEM((2, n, r, t), bf16),
            pltpu.VMEM((n, r, t), bf16),
            pltpu.VMEM((n, rank, c), bf16),
            pltpu.VMEM((n, rank, c), bf16),
            pltpu.VMEM((n + 1, rank, c), f32),
            pltpu.VMEM((n, 2, rank, c), bf16),
            pltpu.VMEM((2, 3, rank, c), f32),
            pltpu.VMEM((n, 2, r, w), bf16),
            pltpu.VMEM((n, 2, r, w), bf16),
            pltpu.VMEM((2, r, d), bf16),
            pltpu.SemaphoreType.DMA((KINDS, 2, n)),
            pltpu.SemaphoreType.DMA((8,)),
        ],
        compiler_params=pltpu.CompilerParams(
            collective_id=0, has_side_effects=True, vmem_limit_bytes=48 * 1024 * 1024
        ),
        cost_estimate=pl.CostEstimate(flops=10**9, bytes_accessed=10**7, transcendentals=0),
    )(tok, cot, down, first, second, up, up_first, up_second)
    columns, up_cast = outs[6], outs[7]
    block = min(256, o)
    merged, *rest = pl.pallas_call(
        merge_kernel,
        grid=(2, o // block),
        out_shape=(
            jax.ShapeDtypeStruct((2, o, w), bf16),
            down_like, down_like, down_like, up_like, up_like, up_like,
        ),
        in_specs=[
            pl.BlockSpec((1, block, w), lambda m, i: (m, i, 0)),
            pl.BlockSpec((1, rank, block), lambda m, i: (m, 0, i)),
            pl.BlockSpec((1, rank, w), lambda m, i: (m, 0, 0)),
        ] + [anywhere] * 6,
        out_specs=(pl.BlockSpec((1, block, w), lambda m, i: (m, i, 0)),) + (anywhere,) * 6,
        scratch_shapes=[pltpu.SemaphoreType.DMA((6,))],
        compiler_params=pltpu.CompilerParams(vmem_limit_bytes=32 * 1024 * 1024),
    )(frozen, up_cast, columns, *outs[:6])
    return (
        merged[None],
        rest[0][None],
        rest[1][None],
        rest[2][None],
        jnp.transpose(rest[3], (2, 0, 1))[None],
        jnp.transpose(rest[4], (2, 0, 1))[None],
        jnp.transpose(rest[5], (2, 0, 1))[None],
    )


def solution(mesh):
    return jax.shard_map(
        functools.partial(local, mesh.shape["dp"]),
        mesh=mesh,
        in_specs=(
            P("pipe", ("groups", "dp"), "sub"),
            P("pipe", ("groups", "dp"), None, None),
            P("pipe", None, None, ("sub", "dp")),
            P("pipe", "dp", "groups", "sub"),
            P("pipe", "dp", "groups", "sub"),
            P("pipe", "dp", "groups", "sub"),
            P("pipe", "dp", "groups", None),
            P("pipe", "dp", "groups", None),
            P("pipe", "dp", "groups", None),
        ),
        out_specs=(
            P("pipe", "groups", None, ("sub", "dp")),
            P("pipe", "dp", "groups", "sub"),
            P("pipe", "dp", "groups", "sub"),
            P("pipe", "dp", "groups", "sub"),
            P("pipe", "dp", "groups", None),
            P("pipe", "dp", "groups", None),
            P("pipe", "dp", "groups", None),
        ),
        check_vma=False,
    )
```

```python
import functools

import jax
import jax.numpy as jnp
from jax import lax
from jax.experimental import pallas as pl
from jax.experimental.pallas import tpu as pltpu
from jax.sharding import PartitionSpec as P

ADAM_STEP = 100

adapter_scale = 2.0
beta_one = 0.9
beta_two = 0.999
learn_rate = 0.005
adam_eps = 1e-08

MESH = pl.DeviceIdType.MESH
UP, UP_CROSS, DOWN, GRAD_DOWN, LOW, GRAD_UP, NEW_UP, NEW_UP_CROSS, STATE, COLUMNS, RELAY = range(11)
KINDS = 11


def apply_adam_rule(current, moment, square, gradient):
    moment_new = beta_one * moment + (1.0 - beta_one) * gradient
    square_new = beta_two * square + (1.0 - beta_two) * gradient * gradient
    fix_first = 1.0 - beta_one**ADAM_STEP
    fix_second = 1.0 - beta_two**ADAM_STEP
    updated = current - learn_rate * (moment_new / fix_first) / (
        jnp.sqrt(square_new / fix_second) + adam_eps
    )
    return (updated, moment_new, square_new)


def exchange_kernel(
    n,
    tok_hbm, cot_hbm, down_hbm, first_hbm, second_hbm, up_hbm, up_first_hbm, up_second_hbm,
    new_down, new_first, new_second, new_up, new_up_first, new_up_second, columns_out, up_out,
    tok, cot_raw, cot, down_raw, first_raw, second_raw, down, first, second, up, up_first, up_second,
    up_all, down_all, back, grad_send, grad_recv, grad_own,
    low_own, low_send, low_recv, gu_send, gu_recv, gu_own, up_new_all, state, col_send, col_all,
    grad_relay, sems, local_sems, out_sems,
):
    bf16, f32 = jnp.bfloat16, jnp.float32
    me = lax.axis_index("dp")
    core = lax.axis_index("sub")
    other = 1 - core
    rows = down.shape[1]
    rank = up.shape[1]
    kv_rows = up.shape[2]
    width = down.shape[2] // n

    def ahead(k):
        return lax.rem(me + k, n)

    def behind(k):
        return lax.rem(me + n - k, n)

    def to_learner(kind, k, src, dst):
        return pltpu.make_async_remote_copy(
            src_ref=src, dst_ref=dst,
            send_sem=sems.at[kind, 0, k], recv_sem=sems.at[kind, 1, k],
            device_id={"dp": ahead(k)}, device_id_type=MESH,
        )

    def to_core(kind, k, src, dst):
        return pltpu.make_async_remote_copy(
            src_ref=src, dst_ref=dst,
            send_sem=sems.at[kind, 0, k], recv_sem=sems.at[kind, 1, k],
            device_id={"sub": other}, device_id_type=MESH,
        )

    relayed = n == 4
    if relayed:
        middle = jnp.logical_and(me > 0, me < 3)
        toward = jnp.where(me < 2, 3, 1)
        near = 4 - toward
        beside = lax.rem(3 * me + 1, 4)

    def loop(lo, hi, body):
        if n <= 4:
            for k in range(lo, hi):
                body(k)
        else:
            lax.fori_loop(lo, hi, lambda k, c: (body(k), c)[1], 0)

    locals_ = [
        pltpu.make_async_copy(src, dst, local_sems.at[i])
        for i, (src, dst) in enumerate(
            (
                (up_hbm, up), (down_hbm, down_raw), (cot_hbm, cot_raw), (tok_hbm, tok),
                (up_first_hbm, up_first), (up_second_hbm, up_second),
                (first_hbm, first_raw), (second_hbm, second_raw),
            )
        )
    ]
    for c in locals_:
        c.start()

    barrier = pltpu.get_barrier_semaphore()
    loop(1, n, lambda k: pl.semaphore_signal(
        barrier, inc=1, device_id={"dp": ahead(k)}, device_id_type=MESH))
    pl.semaphore_signal(barrier, inc=1, device_id={"sub": other}, device_id_type=MESH)

    locals_[0].wait()
    up_all[me] = up[...].astype(bf16)
    pl.semaphore_wait(barrier, n)

    def send_up(k):
        block = up_all.at[me, core]
        to_learner(UP, k, block, block).start()

    def send_down(k):
        block = down_all.at[me]
        to_learner(DOWN, k, block, block).start()

    loop(1, n, send_up)
    locals_[1].wait()
    for m in range(2):
        down[m] = down_raw[:, m, :]
        down_all[me, m] = down[m].astype(bf16)
    if relayed:
        send_down(2)
        for k in (toward, near):
            pl.when(jnp.logical_or(middle, k != toward))(functools.partial(send_down, k))

        @pl.when(jnp.logical_not(middle))
        def _():
            grad_recv[near] = jnp.zeros(grad_recv.shape[1:], bf16)
    else:
        loop(1, n, send_down)

    locals_[2].wait()
    for m in range(2):
        cot[m] = cot_raw[:, m, :]

    def pass_up(k):
        block = up_all.at[behind(k), core]
        to_learner(UP, k, block, block).wait_recv()
        to_core(UP_CROSS, k, block, block).start()

    loop(1, n, pass_up)

    def got_up(k):
        block = up_all.at[behind(k), other]
        to_core(UP_CROSS, k, block, block).wait_recv()

    loop(1, n, got_up)

    for m in range(2):
        total = jnp.zeros((rank, tok.shape[0]), f32)
        for q in range(n):
            total = total + lax.dot_general(
                up_all[q, m], cot[m, :, q * kv_rows:(q + 1) * kv_rows],
                (((1,), (1,)), ((), ())), preferred_element_type=f32)
        total = total.astype(bf16)
        for q in range(n):
            back[q, m] = total[q * rows:(q + 1) * rows]

    locals_[3].wait()

    def grad_for(q):
        lhs = back[q].reshape(2 * rows, tok.shape[0])
        return adapter_scale * jnp.dot(lhs, tok[...], preferred_element_type=f32)

    def send_grad(k):
        q = ahead(k)
        g = grad_for(q).astype(bf16)
        grad_send[k, 0] = g[:rows]
        grad_send[k, 1] = g[rows:]
        to_learner(GRAD_DOWN, k, grad_send.at[k], grad_recv.at[k]).start()

    if relayed:
        relay_in = pltpu.make_async_remote_copy(
            src_ref=grad_send.at[0], dst_ref=grad_relay,
            send_sem=sems.at[RELAY, 0, 0], recv_sem=sems.at[RELAY, 1, 0],
            device_id={"dp": beside}, device_id_type=MESH,
        )

        @pl.when(middle)
        def _():
            send_grad(toward)
            send_grad(near)

        @pl.when(jnp.logical_not(middle))
        def _():
            g = grad_for(ahead(toward)).astype(bf16)
            grad_send[0, 0] = g[:rows]
            grad_send[0, 1] = g[rows:]
            relay_in.start()
            send_grad(2)
            send_grad(near)
    else:
        loop(1, n, send_grad)
    g = grad_for(me)
    grad_own[0] = g[:rows]
    grad_own[1] = g[rows:]
    locals_[6].wait()
    locals_[7].wait()
    for m in range(2):
        first[m] = first_raw[:, m, :]
        second[m] = second_raw[:, m, :]

    def low_for(q):
        part = lax.dot_general(
            down_all[q].reshape(2 * rows, tok.shape[1]), tok[...],
            (((1,), (1,)), ((), ())), preferred_element_type=f32)
        for m in range(2):
            low_own[m, q] = part[m * rows:(m + 1) * rows]
            low_send[m, q] = part[m * rows:(m + 1) * rows].astype(bf16)

    low_for(me)

    def take_down(k):
        q = behind(k)
        block = down_all.at[q]
        to_learner(DOWN, k, block, block).wait_recv()
        low_for(q)

    down_relay = None
    if relayed:
        take_down(2)
        block = down_all.at[behind(2)]
        down_relay = pltpu.make_async_remote_copy(
            src_ref=block, dst_ref=block,
            send_sem=sems.at[RELAY, 0, 1], recv_sem=sems.at[DOWN, 1, lax.rem(2 * me + 3, 4)],
            device_id={"dp": beside}, device_id_type=MESH,
        )

        @pl.when(middle)
        def _():
            down_relay.start()
            g = grad_for(ahead(2))
            relay_in.wait_recv()
            for m in range(2):
                grad_send[2, m] = (
                    g[m * rows:(m + 1) * rows] + grad_relay[m].astype(f32)).astype(bf16)
            to_learner(GRAD_DOWN, 2, grad_send.at[2], grad_recv.at[2]).start()

        take_down(toward)
        take_down(near)
    else:
        loop(1, n, take_down)
    half = to_core(LOW, 0, low_send.at[other], low_recv)
    half.start()
    half.wait()
    lowrank = (low_own[core] + low_recv[...].astype(f32)).astype(bf16).reshape(rank, tok.shape[0])

    gu = adapter_scale * jnp.dot(lowrank, cot[core], preferred_element_type=f32)
    for q in range(n):
        gu_own[q] = gu[:, q * kv_rows:(q + 1) * kv_rows]
        gu_send[q] = gu[:, q * kv_rows:(q + 1) * kv_rows].astype(bf16)

    loop(1, n, lambda k: to_learner(GRAD_UP, k, gu_send.at[ahead(k)], gu_recv.at[k]).start())
    gu_own[n] = gu_own[me]

    def add_up(k):
        to_learner(GRAD_UP, k, gu_send.at[ahead(k)], gu_recv.at[k]).wait_recv()
        gu_own[n] = gu_own[n] + gu_recv[k].astype(f32)

    loop(1, n, add_up)
    locals_[4].wait()
    locals_[5].wait()
    p, f, s = apply_adam_rule(up[core], up_first[core], up_second[core], gu_own[n])
    up_new_all[me, core] = p.astype(bf16)

    def send_new_up(k):
        block = up_new_all.at[me, core]
        to_learner(NEW_UP, k, block, block).start()

    loop(1, n, send_new_up)
    state[core, 0] = p
    state[core, 1] = f
    state[core, 2] = s
    mine = to_core(STATE, 0, state.at[core], state.at[core])
    mine.start()

    def got_grad(k):
        to_learner(GRAD_DOWN, k, grad_send.at[k], grad_recv.at[k]).wait_recv()

    if relayed:
        got_grad(2)
        got_grad(toward)
        pl.when(middle)(functools.partial(got_grad, near))
    else:
        loop(1, n, got_grad)

    def adam_down(k):
        q = ahead(k)
        cols = pl.ds(pl.multiple_of(q * width, 128), width)
        for m in range(2):
            g = grad_own[m, :, cols]
            for j in range(1, n):
                g = g + grad_recv[j, m, :, cols].astype(f32)
            p, f, s = apply_adam_rule(down[m, :, cols], first[m, :, cols], second[m, :, cols], g)
            down[m, :, cols] = p
            first[m, :, cols] = f
            second[m, :, cols] = s
            if isinstance(k, int) and k == 0:
                col_all[me, m] = p.astype(bf16)
            else:
                col_send[k, m] = p.astype(bf16)

    def send_columns(k):
        adam_down(k)
        to_learner(COLUMNS, k, col_send.at[k], col_all.at[me]).start()

    if relayed:
        send_columns(2)
        send_columns(toward)
        send_columns(near)
    else:
        loop(1, n, send_columns)
    adam_down(0)

    def pass_new_up(k):
        block = up_new_all.at[behind(k), core]
        to_learner(NEW_UP, k, block, block).wait_recv()
        to_core(NEW_UP_CROSS, k, block, block).start()

    loop(1, n, pass_new_up)
    outputs = []

    def write_out(src, dst):
        outputs.append(pltpu.make_async_copy(src, dst, out_sems.at[len(outputs)]))
        outputs[-1].start()

    to_core(STATE, 0, state.at[other], state.at[other]).wait_recv()
    for m in range(2):
        for i, out in enumerate((new_up, new_up_first, new_up_second)):
            write_out(state.at[m, i], out.at[m])
    up_new_all[me, other] = state[other, 0].astype(bf16)

    for new, raw, out in (
        (down, down_raw, new_down), (first, first_raw, new_first), (second, second_raw, new_second)
    ):
        for m in range(2):
            raw[:, m, :] = new[m]
        write_out(raw, out)

    def got_new_up(k):
        block = up_new_all.at[behind(k), other]
        to_core(NEW_UP_CROSS, k, block, block).wait_recv()

    loop(1, n, got_new_up)
    write_out(up_new_all, up_out)

    def got_columns(k):
        to_learner(COLUMNS, k, col_send.at[k], col_all.at[behind(k)]).wait_recv()

    loop(1, n, got_columns)
    write_out(col_all, columns_out)

    def sent(k):
        block = up_all.at[me, core]
        to_learner(UP, k, block, block).wait_send()
        block = up_all.at[behind(k), core]
        to_core(UP_CROSS, k, block, block).wait_send()
        to_learner(GRAD_UP, k, gu_send.at[ahead(k)], gu_recv.at[k]).wait_send()
        block = up_new_all.at[me, core]
        to_learner(NEW_UP, k, block, block).wait_send()
        block = up_new_all.at[behind(k), core]
        to_core(NEW_UP_CROSS, k, block, block).wait_send()
        to_learner(COLUMNS, k, col_send.at[k], col_all.at[me]).wait_send()

    def sent_down(k):
        block = down_all.at[me]
        to_learner(DOWN, k, block, block).wait_send()
        to_learner(GRAD_DOWN, k, grad_send.at[k], grad_recv.at[k]).wait_send()

    loop(1, n, sent)
    if relayed:
        sent_down(2)
        sent_down(near)

        @pl.when(middle)
        def _():
            sent_down(toward)
            down_relay.wait_send()

        @pl.when(jnp.logical_not(middle))
        def _():
            relay_in.wait_send()
    else:
        loop(1, n, sent_down)
    mine.wait_send()
    for c in outputs:
        c.wait()


def merge_kernel(
    frozen, up, columns, d0, d1, d2, u0, u1, u2,
    merged, e0, e1, e2, v0, v1, v2, sems,
):
    step = pl.program_id(0) * pl.num_programs(1) + pl.program_id(1)
    last = pl.num_programs(0) * pl.num_programs(1) - 1
    pairs = ((d0, e0), (d1, e1), (d2, e2), (u0, v0), (u1, v1), (u2, v2))
    copies = [pltpu.make_async_copy(a, b, sems.at[i]) for i, (a, b) in enumerate(pairs)]

    @pl.when(step == 0)
    def _():
        for c in copies:
            c.start()

    n, _, rows, width = columns.shape
    change = lax.dot_general(
        adapter_scale * up[0, 0], columns[:, 0].reshape(n * rows, width),
        (((0,), (0,)), ((), ())), preferred_element_type=jnp.float32)
    merged[0] = (frozen[0].astype(jnp.float32) + change).astype(merged.dtype)

    @pl.when(step == last)
    def _():
        for c in copies:
            c.wait()


def local(
    n,
    tokens,
    cotangent,
    frozen_weight,
    adapter_down,
    down_first_moment,
    down_second_moment,
    adapter_up,
    up_first_moment,
    up_second_moment,
):
    bf16, f32 = jnp.bfloat16, jnp.float32
    tok, cot, frozen = tokens[0], cotangent[0], frozen_weight[0]
    down, first, second = adapter_down[0], down_first_moment[0], down_second_moment[0]
    up, up_first, up_second = [
        jnp.transpose(a[0], (1, 2, 0)) for a in (adapter_up, up_first_moment, up_second_moment)
    ]
    t, d = tok.shape
    _, kinds, o = cot.shape
    r = down.shape[0]
    rank, c = up.shape[1:]
    w = d // n
    hbm = pl.BlockSpec(memory_space=pltpu.HBM)
    down_like = jax.ShapeDtypeStruct(down.shape, f32)
    up_like = jax.ShapeDtypeStruct(up.shape, f32)
    outs = pl.pallas_call(
        functools.partial(exchange_kernel, n),
        out_shape=(
            down_like, down_like, down_like, up_like, up_like, up_like,
            jax.ShapeDtypeStruct((n, 2, r, w), bf16),
            jax.ShapeDtypeStruct((n, 2, rank, c), bf16),
        ),
        in_specs=[hbm] * 8,
        out_specs=(hbm,) * 8,
        scratch_shapes=[
            pltpu.VMEM((t, d), bf16),
            pltpu.VMEM((t, 2, o), bf16),
            pltpu.VMEM((2, t, o), bf16),
            pltpu.VMEM((r, 2, d), f32),
            pltpu.VMEM((r, 2, d), f32),
            pltpu.VMEM((r, 2, d), f32),
            pltpu.VMEM((2, r, d), f32),
            pltpu.VMEM((2, r, d), f32),
            pltpu.VMEM((2, r, d), f32),
            pltpu.VMEM((2, rank, c), f32),
            pltpu.VMEM((2, rank, c), f32),
            pltpu.VMEM((2, rank, c), f32),
            pltpu.VMEM((n, 2, rank, c), bf16),
            pltpu.VMEM((n, 2, r, d), bf16),
            pltpu.VMEM((n, 2, r, t), bf16),
            pltpu.VMEM((n, 2, r, d), bf16),
            pltpu.VMEM((n, 2, r, d), bf16),
            pltpu.VMEM((2, r, d), f32),
            pltpu.VMEM((2, n, r, t), f32),
            pltpu.VMEM((2, n, r, t), bf16),
            pltpu.VMEM((n, r, t), bf16),
            pltpu.VMEM((n, rank, c), bf16),
            pltpu.VMEM((n, rank, c), bf16),
            pltpu.VMEM((n + 1, rank, c), f32),
            pltpu.VMEM((n, 2, rank, c), bf16),
            pltpu.VMEM((2, 3, rank, c), f32),
            pltpu.VMEM((n, 2, r, w), bf16),
            pltpu.VMEM((n, 2, r, w), bf16),
            pltpu.VMEM((2, r, d), bf16),
            pltpu.SemaphoreType.DMA((KINDS, 2, n)),
            pltpu.SemaphoreType.DMA((8,)),
            pltpu.SemaphoreType.DMA((11,)),
        ],
        compiler_params=pltpu.CompilerParams(
            collective_id=0, has_side_effects=True, vmem_limit_bytes=60 * 1024 * 1024
        ),
        cost_estimate=pl.CostEstimate(flops=10**9, bytes_accessed=10**7, transcendentals=0),
    )(tok, cot, down, first, second, up, up_first, up_second)
    columns, up_cast = outs[6], outs[7]
    merged, *rest = pl.pallas_call(
        merge_kernel,
        grid=(2, n),
        out_shape=(
            jax.ShapeDtypeStruct((2, o, w), bf16),
            down_like, down_like, down_like, up_like, up_like, up_like,
        ),
        in_specs=[
            pl.BlockSpec((1, c, w), lambda m, i: (m, i, 0)),
            pl.BlockSpec((1, 1, rank, c), lambda m, i: (i, m, 0, 0)),
            pl.BlockSpec((n, 1, r, w), lambda m, i: (0, m, 0, 0)),
        ] + [hbm] * 6,
        out_specs=(pl.BlockSpec((1, c, w), lambda m, i: (m, i, 0)),) + (hbm,) * 6,
        scratch_shapes=[pltpu.SemaphoreType.DMA((6,))],
        compiler_params=pltpu.CompilerParams(vmem_limit_bytes=60 * 1024 * 1024),
    )(frozen, up_cast, columns, *outs[:6])
    return (
        merged[None],
        rest[0][None],
        rest[1][None],
        rest[2][None],
        jnp.transpose(rest[3], (2, 0, 1))[None],
        jnp.transpose(rest[4], (2, 0, 1))[None],
        jnp.transpose(rest[5], (2, 0, 1))[None],
    )


def solution(mesh):
    return jax.shard_map(
        functools.partial(local, mesh.shape["dp"]),
        mesh=mesh,
        in_specs=(
            P("pipe", ("groups", "dp"), "sub"),
            P("pipe", ("groups", "dp"), None, None),
            P("pipe", None, None, ("sub", "dp")),
            P("pipe", "dp", "groups", "sub"),
            P("pipe", "dp", "groups", "sub"),
            P("pipe", "dp", "groups", "sub"),
            P("pipe", "dp", "groups", None),
            P("pipe", "dp", "groups", None),
            P("pipe", "dp", "groups", None),
        ),
        out_specs=(
            P("pipe", "groups", None, ("sub", "dp")),
            P("pipe", "dp", "groups", "sub"),
            P("pipe", "dp", "groups", "sub"),
            P("pipe", "dp", "groups", "sub"),
            P("pipe", "dp", "groups", None),
            P("pipe", "dp", "groups", None),
            P("pipe", "dp", "groups", None),
        ),
        check_vma=False,
    )
```

```python
import functools

import jax
import jax.numpy as jnp
from jax import lax
from jax.experimental import pallas as pl
from jax.experimental.pallas import tpu as pltpu
from jax.sharding import PartitionSpec as P

ADAM_STEP = 100

adapter_scale = 2.0
beta_one = 0.9
beta_two = 0.999
learn_rate = 0.005
adam_eps = 1e-08

MESH = pl.DeviceIdType.MESH
UP, UP_CROSS, DOWN, GRAD_DOWN, LOW, GRAD_UP, NEW_UP, NEW_UP_CROSS, STATE, COLUMNS, RELAY = range(11)
KINDS = 11


def apply_adam_rule(current, moment, square, gradient):
    moment_new = beta_one * moment + (1.0 - beta_one) * gradient
    square_new = beta_two * square + (1.0 - beta_two) * gradient * gradient
    fix_first = 1.0 - beta_one**ADAM_STEP
    fix_second = 1.0 - beta_two**ADAM_STEP
    updated = current - learn_rate * (moment_new / fix_first) / (
        jnp.sqrt(square_new / fix_second) + adam_eps
    )
    return (updated, moment_new, square_new)


def exchange_kernel(
    n,
    tok_hbm, cot_hbm, down_hbm, first_hbm, second_hbm, up_hbm, up_first_hbm, up_second_hbm,
    new_down, new_first, new_second, new_up, new_up_first, new_up_second, columns_out, up_out,
    tok, cot_raw, cot, down_raw, first_raw, second_raw, down, first, second, up, up_first, up_second,
    up_all, down_all, back, grad_send, grad_recv, grad_own,
    low_own, low_send, low_recv, gu_send, gu_recv, gu_own, up_new_all, state, col_send, col_all,
    grad_relay, sems, local_sems, out_sems,
):
    bf16, f32 = jnp.bfloat16, jnp.float32
    me = lax.axis_index("dp")
    core = lax.axis_index("sub")
    other = 1 - core
    rows = down.shape[1]
    rank = up.shape[1]
    kv_rows = up.shape[2]
    width = down.shape[2] // n

    def ahead(k):
        return lax.rem(me + k, n)

    def behind(k):
        return lax.rem(me + n - k, n)

    def to_learner(kind, k, src, dst):
        return pltpu.make_async_remote_copy(
            src_ref=src, dst_ref=dst,
            send_sem=sems.at[kind, 0, k], recv_sem=sems.at[kind, 1, k],
            device_id={"dp": ahead(k)}, device_id_type=MESH,
        )

    def to_core(kind, k, src, dst):
        return pltpu.make_async_remote_copy(
            src_ref=src, dst_ref=dst,
            send_sem=sems.at[kind, 0, k], recv_sem=sems.at[kind, 1, k],
            device_id={"sub": other}, device_id_type=MESH,
        )

    relayed = n == 4
    if relayed:
        middle = jnp.logical_and(me > 0, me < 3)
        toward = jnp.where(me < 2, 3, 1)
        near = 4 - toward
        beside = lax.rem(3 * me + 1, 4)

    def loop(lo, hi, body):
        if n <= 4:
            for k in range(lo, hi):
                body(k)
        else:
            lax.fori_loop(lo, hi, lambda k, c: (body(k), c)[1], 0)

    locals_ = [
        pltpu.make_async_copy(src, dst, local_sems.at[i])
        for i, (src, dst) in enumerate(
            (
                (up_hbm, up), (down_hbm, down_raw), (cot_hbm, cot_raw), (tok_hbm, tok),
                (up_first_hbm, up_first), (up_second_hbm, up_second),
                (first_hbm, first_raw), (second_hbm, second_raw),
            )
        )
    ]
    for c in locals_:
        c.start()

    barrier = pltpu.get_barrier_semaphore()
    loop(1, n, lambda k: pl.semaphore_signal(
        barrier, inc=1, device_id={"dp": ahead(k)}, device_id_type=MESH))
    pl.semaphore_signal(barrier, inc=1, device_id={"sub": other}, device_id_type=MESH)

    locals_[0].wait()
    up_all[me] = up[...].astype(bf16)
    pl.semaphore_wait(barrier, n)

    def send_up(k):
        block = up_all.at[me, core]
        to_learner(UP, k, block, block).start()

    def send_down(k):
        block = down_all.at[me]
        to_learner(DOWN, k, block, block).start()

    loop(1, n, send_up)
    locals_[1].wait()
    for m in range(2):
        down[m] = down_raw[:, m, :]
        down_all[me, m] = down[m].astype(bf16)
    if relayed:
        send_down(2)
        for k in (toward, near):
            pl.when(jnp.logical_or(middle, k != toward))(functools.partial(send_down, k))

        @pl.when(jnp.logical_not(middle))
        def _():
            grad_recv[near] = jnp.zeros(grad_recv.shape[1:], bf16)
    else:
        loop(1, n, send_down)

    locals_[2].wait()
    for m in range(2):
        cot[m] = cot_raw[:, m, :]

    def pass_up(k):
        block = up_all.at[behind(k), core]
        to_learner(UP, k, block, block).wait_recv()
        to_core(UP_CROSS, k, block, block).start()

    loop(1, n, pass_up)

    def got_up(k):
        block = up_all.at[behind(k), other]
        to_core(UP_CROSS, k, block, block).wait_recv()

    loop(1, n, got_up)

    for m in range(2):
        total = jnp.zeros((rank, tok.shape[0]), f32)
        for q in range(n):
            total = total + lax.dot_general(
                up_all[q, m], cot[m, :, q * kv_rows:(q + 1) * kv_rows],
                (((1,), (1,)), ((), ())), preferred_element_type=f32)
        total = total.astype(bf16)
        for q in range(n):
            back[q, m] = total[q * rows:(q + 1) * rows]

    locals_[3].wait()

    def grad_for(q):
        lhs = back[q].reshape(2 * rows, tok.shape[0])
        return adapter_scale * jnp.dot(lhs, tok[...], preferred_element_type=f32)

    def send_grad(k):
        q = ahead(k)
        g = grad_for(q).astype(bf16)
        grad_send[k, 0] = g[:rows]
        grad_send[k, 1] = g[rows:]
        to_learner(GRAD_DOWN, k, grad_send.at[k], grad_recv.at[k]).start()

    if relayed:
        relay_in = pltpu.make_async_remote_copy(
            src_ref=grad_send.at[0], dst_ref=grad_relay,
            send_sem=sems.at[RELAY, 0, 0], recv_sem=sems.at[RELAY, 1, 0],
            device_id={"dp": beside}, device_id_type=MESH,
        )

        @pl.when(middle)
        def _():
            send_grad(toward)
            send_grad(near)

        @pl.when(jnp.logical_not(middle))
        def _():
            g = grad_for(ahead(toward)).astype(bf16)
            grad_send[0, 0] = g[:rows]
            grad_send[0, 1] = g[rows:]
            relay_in.start()
            send_grad(2)
            send_grad(near)
    else:
        loop(1, n, send_grad)
    g = grad_for(me)
    grad_own[0] = g[:rows]
    grad_own[1] = g[rows:]
    locals_[6].wait()
    locals_[7].wait()
    for m in range(2):
        first[m] = first_raw[:, m, :]
        second[m] = second_raw[:, m, :]

    def low_for(q):
        part = lax.dot_general(
            down_all[q].reshape(2 * rows, tok.shape[1]), tok[...],
            (((1,), (1,)), ((), ())), preferred_element_type=f32)
        for m in range(2):
            low_own[m, q] = part[m * rows:(m + 1) * rows]
            low_send[m, q] = part[m * rows:(m + 1) * rows].astype(bf16)

    low_for(me)

    def take_down(k):
        q = behind(k)
        block = down_all.at[q]
        to_learner(DOWN, k, block, block).wait_recv()
        low_for(q)

    down_relay = None
    if relayed:
        take_down(2)
        block = down_all.at[behind(2)]
        down_relay = pltpu.make_async_remote_copy(
            src_ref=block, dst_ref=block,
            send_sem=sems.at[RELAY, 0, 1], recv_sem=sems.at[DOWN, 1, lax.rem(2 * me + 3, 4)],
            device_id={"dp": beside}, device_id_type=MESH,
        )

        @pl.when(middle)
        def _():
            down_relay.start()
            g = grad_for(ahead(2))
            relay_in.wait_recv()
            for m in range(2):
                grad_send[2, m] = (
                    g[m * rows:(m + 1) * rows] + grad_relay[m].astype(f32)).astype(bf16)
            to_learner(GRAD_DOWN, 2, grad_send.at[2], grad_recv.at[2]).start()

        take_down(toward)
        take_down(near)
    else:
        loop(1, n, take_down)
    half = to_core(LOW, 0, low_send.at[other], low_recv)
    half.start()
    half.wait()
    lowrank = (low_own[core] + low_recv[...].astype(f32)).astype(bf16).reshape(rank, tok.shape[0])

    gu = adapter_scale * jnp.dot(lowrank, cot[core], preferred_element_type=f32)
    for q in range(n):
        gu_own[q] = gu[:, q * kv_rows:(q + 1) * kv_rows]
        gu_send[q] = gu[:, q * kv_rows:(q + 1) * kv_rows].astype(bf16)

    loop(1, n, lambda k: to_learner(GRAD_UP, k, gu_send.at[ahead(k)], gu_recv.at[k]).start())
    gu_own[n] = gu_own[me]

    def add_up(k):
        to_learner(GRAD_UP, k, gu_send.at[ahead(k)], gu_recv.at[k]).wait_recv()
        gu_own[n] = gu_own[n] + gu_recv[k].astype(f32)

    loop(1, n, add_up)
    locals_[4].wait()
    locals_[5].wait()
    p, f, s = apply_adam_rule(up[core], up_first[core], up_second[core], gu_own[n])
    up_new_all[me, core] = p.astype(bf16)

    def send_new_up(k):
        block = up_new_all.at[me, core]
        to_learner(NEW_UP, k, block, block).start()

    loop(1, n, send_new_up)
    state[core, 0] = p
    state[core, 1] = f
    state[core, 2] = s
    mine = to_core(STATE, 0, state.at[core], state.at[core])
    mine.start()

    def got_grad(k):
        to_learner(GRAD_DOWN, k, grad_send.at[k], grad_recv.at[k]).wait_recv()

    if relayed:
        got_grad(2)
        got_grad(toward)
        pl.when(middle)(functools.partial(got_grad, near))
    else:
        loop(1, n, got_grad)

    def adam_down(k):
        q = ahead(k)
        cols = pl.ds(pl.multiple_of(q * width, 128), width)
        for m in range(2):
            g = grad_own[m, :, cols]
            for j in range(1, n):
                g = g + grad_recv[j, m, :, cols].astype(f32)
            p, f, s = apply_adam_rule(down[m, :, cols], first[m, :, cols], second[m, :, cols], g)
            down[m, :, cols] = p
            first[m, :, cols] = f
            second[m, :, cols] = s
            if isinstance(k, int) and k == 0:
                col_all[me, m] = p.astype(bf16)
            else:
                col_send[k, m] = p.astype(bf16)

    def send_columns(k):
        adam_down(k)
        to_learner(COLUMNS, k, col_send.at[k], col_all.at[me]).start()

    if relayed:
        send_columns(2)
        send_columns(toward)
        send_columns(near)
    else:
        loop(1, n, send_columns)
    adam_down(0)

    def pass_new_up(k):
        block = up_new_all.at[behind(k), core]
        to_learner(NEW_UP, k, block, block).wait_recv()
        to_core(NEW_UP_CROSS, k, block, block).start()

    loop(1, n, pass_new_up)
    outputs = []

    def write_out(src, dst):
        outputs.append(pltpu.make_async_copy(src, dst, out_sems.at[len(outputs)]))
        outputs[-1].start()

    to_core(STATE, 0, state.at[other], state.at[other]).wait_recv()
    for m in range(2):
        for i, out in enumerate((new_up, new_up_first, new_up_second)):
            write_out(state.at[m, i], out.at[m])
    up_new_all[me, other] = state[other, 0].astype(bf16)

    for new, raw, out in (
        (down, down_raw, new_down), (first, first_raw, new_first), (second, second_raw, new_second)
    ):
        for m in range(2):
            raw[:, m, :] = new[m]
        write_out(raw, out)

    def got_new_up(k):
        block = up_new_all.at[behind(k), other]
        to_core(NEW_UP_CROSS, k, block, block).wait_recv()

    loop(1, n, got_new_up)
    write_out(up_new_all, up_out)

    def got_columns(k):
        to_learner(COLUMNS, k, col_send.at[k], col_all.at[behind(k)]).wait_recv()

    loop(1, n, got_columns)
    write_out(col_all, columns_out)

    def sent(k):
        block = up_all.at[me, core]
        to_learner(UP, k, block, block).wait_send()
        block = up_all.at[behind(k), core]
        to_core(UP_CROSS, k, block, block).wait_send()
        to_learner(GRAD_UP, k, gu_send.at[ahead(k)], gu_recv.at[k]).wait_send()
        block = up_new_all.at[me, core]
        to_learner(NEW_UP, k, block, block).wait_send()
        block = up_new_all.at[behind(k), core]
        to_core(NEW_UP_CROSS, k, block, block).wait_send()
        to_learner(COLUMNS, k, col_send.at[k], col_all.at[me]).wait_send()

    def sent_down(k):
        block = down_all.at[me]
        to_learner(DOWN, k, block, block).wait_send()
        to_learner(GRAD_DOWN, k, grad_send.at[k], grad_recv.at[k]).wait_send()

    loop(1, n, sent)
    if relayed:
        sent_down(2)
        sent_down(near)

        @pl.when(middle)
        def _():
            sent_down(toward)
            down_relay.wait_send()

        @pl.when(jnp.logical_not(middle))
        def _():
            relay_in.wait_send()
    else:
        loop(1, n, sent_down)
    mine.wait_send()
    for c in outputs:
        c.wait()


def merge_kernel(
    frozen, up, columns, d0, d1, d2, u0, u1, u2,
    merged, e0, e1, e2, v0, v1, v2, b0, b1, b2, b3, b4, b5, sems,
):
    step = pl.program_id(0) * pl.num_programs(1) + pl.program_id(1)
    last = pl.num_programs(0) * pl.num_programs(1) - 1
    loads = [
        pltpu.make_async_copy(a, b, sems.at[0, i])
        for i, (a, b) in enumerate(((d0, b0), (d1, b1), (d2, b2), (u0, b3), (u1, b4), (u2, b5)))
    ]
    stores = [
        pltpu.make_async_copy(b, a, sems.at[1, i])
        for i, (a, b) in enumerate(((e0, b0), (e1, b1), (e2, b2), (v0, b3), (v1, b4), (v2, b5)))
    ]

    @pl.when(step == 0)
    def _():
        for c in loads:
            c.start()

    @pl.when(step == 1)
    def _():
        for c, e in zip(loads, stores):
            c.wait()
            e.start()

    n, _, rows, width = columns.shape
    change = lax.dot_general(
        adapter_scale * up[0, 0], columns[:, 0].reshape(n * rows, width),
        (((0,), (0,)), ((), ())), preferred_element_type=jnp.float32)
    merged[0] = (frozen[0].astype(jnp.float32) + change).astype(merged.dtype)

    @pl.when(step == last)
    def _():
        for c in stores:
            c.wait()


def local(
    n,
    tokens,
    cotangent,
    frozen_weight,
    adapter_down,
    down_first_moment,
    down_second_moment,
    adapter_up,
    up_first_moment,
    up_second_moment,
):
    bf16, f32 = jnp.bfloat16, jnp.float32
    tok, cot, frozen = tokens[0], cotangent[0], frozen_weight[0]
    down, first, second = adapter_down[0], down_first_moment[0], down_second_moment[0]
    up, up_first, up_second = [
        jnp.transpose(a[0], (1, 2, 0)) for a in (adapter_up, up_first_moment, up_second_moment)
    ]
    t, d = tok.shape
    _, kinds, o = cot.shape
    r = down.shape[0]
    rank, c = up.shape[1:]
    w = d // n
    hbm = pl.BlockSpec(memory_space=pltpu.HBM)
    down_like = jax.ShapeDtypeStruct(down.shape, f32)
    up_like = jax.ShapeDtypeStruct(up.shape, f32)
    outs = pl.pallas_call(
        functools.partial(exchange_kernel, n),
        out_shape=(
            down_like, down_like, down_like, up_like, up_like, up_like,
            jax.ShapeDtypeStruct((n, 2, r, w), bf16),
            jax.ShapeDtypeStruct((n, 2, rank, c), bf16),
        ),
        in_specs=[hbm] * 8,
        out_specs=(hbm,) * 8,
        scratch_shapes=[
            pltpu.VMEM((t, d), bf16),
            pltpu.VMEM((t, 2, o), bf16),
            pltpu.VMEM((2, t, o), bf16),
            pltpu.VMEM((r, 2, d), f32),
            pltpu.VMEM((r, 2, d), f32),
            pltpu.VMEM((r, 2, d), f32),
            pltpu.VMEM((2, r, d), f32),
            pltpu.VMEM((2, r, d), f32),
            pltpu.VMEM((2, r, d), f32),
            pltpu.VMEM((2, rank, c), f32),
            pltpu.VMEM((2, rank, c), f32),
            pltpu.VMEM((2, rank, c), f32),
            pltpu.VMEM((n, 2, rank, c), bf16),
            pltpu.VMEM((n, 2, r, d), bf16),
            pltpu.VMEM((n, 2, r, t), bf16),
            pltpu.VMEM((n, 2, r, d), bf16),
            pltpu.VMEM((n, 2, r, d), bf16),
            pltpu.VMEM((2, r, d), f32),
            pltpu.VMEM((2, n, r, t), f32),
            pltpu.VMEM((2, n, r, t), bf16),
            pltpu.VMEM((n, r, t), bf16),
            pltpu.VMEM((n, rank, c), bf16),
            pltpu.VMEM((n, rank, c), bf16),
            pltpu.VMEM((n + 1, rank, c), f32),
            pltpu.VMEM((n, 2, rank, c), bf16),
            pltpu.VMEM((2, 3, rank, c), f32),
            pltpu.VMEM((n, 2, r, w), bf16),
            pltpu.VMEM((n, 2, r, w), bf16),
            pltpu.VMEM((2, r, d), bf16),
            pltpu.SemaphoreType.DMA((KINDS, 2, n)),
            pltpu.SemaphoreType.DMA((8,)),
            pltpu.SemaphoreType.DMA((11,)),
        ],
        compiler_params=pltpu.CompilerParams(
            collective_id=0, has_side_effects=True, vmem_limit_bytes=60 * 1024 * 1024
        ),
        cost_estimate=pl.CostEstimate(flops=10**9, bytes_accessed=10**7, transcendentals=0),
    )(tok, cot, down, first, second, up, up_first, up_second)
    columns, up_cast = outs[6], outs[7]
    merged, *rest = pl.pallas_call(
        merge_kernel,
        grid=(2, n),
        out_shape=(
            jax.ShapeDtypeStruct((2, o, w), bf16),
            down_like, down_like, down_like, up_like, up_like, up_like,
        ),
        in_specs=[
            pl.BlockSpec((1, c, w), lambda m, i: (m, i, 0)),
            pl.BlockSpec((1, 1, rank, c), lambda m, i: (i, m, 0, 0)),
            pl.BlockSpec((n, 1, r, w), lambda m, i: (0, m, 0, 0)),
        ] + [hbm] * 6,
        out_specs=(pl.BlockSpec((1, c, w), lambda m, i: (m, i, 0)),) + (hbm,) * 6,
        scratch_shapes=[pltpu.VMEM(down.shape, f32)] * 3 + [pltpu.VMEM(up.shape, f32)] * 3 + [
            pltpu.SemaphoreType.DMA((2, 6))
        ],
        compiler_params=pltpu.CompilerParams(vmem_limit_bytes=60 * 1024 * 1024),
    )(frozen, up_cast, columns, *outs[:6])
    return (
        merged[None],
        rest[0][None],
        rest[1][None],
        rest[2][None],
        jnp.transpose(rest[3], (2, 0, 1))[None],
        jnp.transpose(rest[4], (2, 0, 1))[None],
        jnp.transpose(rest[5], (2, 0, 1))[None],
    )


def solution(mesh):
    return jax.shard_map(
        functools.partial(local, mesh.shape["dp"]),
        mesh=mesh,
        in_specs=(
            P("pipe", ("groups", "dp"), "sub"),
            P("pipe", ("groups", "dp"), None, None),
            P("pipe", None, None, ("sub", "dp")),
            P("pipe", "dp", "groups", "sub"),
            P("pipe", "dp", "groups", "sub"),
            P("pipe", "dp", "groups", "sub"),
            P("pipe", "dp", "groups", None),
            P("pipe", "dp", "groups", None),
            P("pipe", "dp", "groups", None),
        ),
        out_specs=(
            P("pipe", "groups", None, ("sub", "dp")),
            P("pipe", "dp", "groups", "sub"),
            P("pipe", "dp", "groups", "sub"),
            P("pipe", "dp", "groups", "sub"),
            P("pipe", "dp", "groups", None),
            P("pipe", "dp", "groups", None),
            P("pipe", "dp", "groups", None),
        ),
        check_vma=False,
    )
```

```python
import functools

import jax
import jax.numpy as jnp
from jax import lax
from jax.experimental import pallas as pl
from jax.experimental.pallas import tpu as pltpu
from jax.sharding import PartitionSpec as P

ADAM_STEP = 100

adapter_scale = 2.0
beta_one = 0.9
beta_two = 0.999
learn_rate = 0.005
adam_eps = 1e-08

MESH = pl.DeviceIdType.MESH
UP, UP_CROSS, DOWN, GRAD_DOWN, LOW, GRAD_UP, NEW_UP, NEW_UP_CROSS, STATE, COLUMNS, RELAY = range(11)
KINDS = 11


def apply_adam_rule(current, moment, square, gradient):
    moment_new = beta_one * moment + (1.0 - beta_one) * gradient
    square_new = beta_two * square + (1.0 - beta_two) * gradient * gradient
    fix_first = 1.0 - beta_one**ADAM_STEP
    fix_second = 1.0 - beta_two**ADAM_STEP
    updated = current - learn_rate * (moment_new / fix_first) / (
        jnp.sqrt(square_new / fix_second) + adam_eps
    )
    return (updated, moment_new, square_new)


def exchange_kernel(
    n,
    tok_hbm, cot_hbm, down_hbm, first_hbm, second_hbm, up_hbm, up_first_hbm, up_second_hbm,
    new_down, new_first, new_second, new_up, new_up_first, new_up_second, columns_out, up_out,
    tok, cot_raw, cot, down_raw, first_raw, second_raw, down, first, second, up, up_first, up_second,
    up_all, down_all, back, grad_send, grad_recv, grad_own,
    low_own, low_send, low_recv, gu_send, gu_recv, gu_own, up_new_all, state, col_send, col_all,
    grad_relay, sems, local_sems, out_sems,
):
    bf16, f32 = jnp.bfloat16, jnp.float32
    me = lax.axis_index("dp")
    core = lax.axis_index("sub")
    other = 1 - core
    rows = down.shape[1]
    rank = up.shape[1]
    kv_rows = up.shape[2]
    width = down.shape[2] // n

    def ahead(k):
        return lax.rem(me + k, n)

    def behind(k):
        return lax.rem(me + n - k, n)

    def to_learner(kind, k, src, dst):
        return pltpu.make_async_remote_copy(
            src_ref=src, dst_ref=dst,
            send_sem=sems.at[kind, 0, k], recv_sem=sems.at[kind, 1, k],
            device_id={"dp": ahead(k)}, device_id_type=MESH,
        )

    def to_core(kind, k, src, dst):
        return pltpu.make_async_remote_copy(
            src_ref=src, dst_ref=dst,
            send_sem=sems.at[kind, 0, k], recv_sem=sems.at[kind, 1, k],
            device_id={"sub": other}, device_id_type=MESH,
        )

    relayed = n == 4
    if relayed:
        middle = jnp.logical_and(me > 0, me < 3)
        toward = jnp.where(me < 2, 3, 1)
        near = 4 - toward
        beside = lax.rem(3 * me + 1, 4)

    def loop(lo, hi, body):
        if n <= 4:
            for k in range(lo, hi):
                body(k)
        else:
            lax.fori_loop(lo, hi, lambda k, c: (body(k), c)[1], 0)

    locals_ = [
        pltpu.make_async_copy(src, dst, local_sems.at[i])
        for i, (src, dst) in enumerate(
            (
                (up_hbm, up), (down_hbm, down_raw), (cot_hbm, cot_raw), (tok_hbm, tok),
                (up_first_hbm, up_first), (up_second_hbm, up_second),
                (first_hbm, first_raw), (second_hbm, second_raw),
            )
        )
    ]
    for c in locals_:
        c.start()

    barrier = pltpu.get_barrier_semaphore()
    loop(1, n, lambda k: pl.semaphore_signal(
        barrier, inc=1, device_id={"dp": ahead(k)}, device_id_type=MESH))
    pl.semaphore_signal(barrier, inc=1, device_id={"sub": other}, device_id_type=MESH)

    locals_[0].wait()
    up_all[me] = up[...].astype(bf16)
    pl.semaphore_wait(barrier, n)

    def send_up(k):
        block = up_all.at[me, core]
        to_learner(UP, k, block, block).start()

    def send_down(k):
        block = down_all.at[me]
        to_learner(DOWN, k, block, block).start()

    loop(1, n, send_up)
    locals_[1].wait()
    for m in range(2):
        down[m] = down_raw[:, m, :]
        down_all[me, m] = down[m].astype(bf16)
    if relayed:
        send_down(2)
        for k in (toward, near):
            pl.when(jnp.logical_or(middle, k != toward))(functools.partial(send_down, k))

        @pl.when(jnp.logical_not(middle))
        def _():
            grad_recv[near] = jnp.zeros(grad_recv.shape[1:], bf16)
    else:
        loop(1, n, send_down)

    locals_[2].wait()
    for m in range(2):
        cot[m] = cot_raw[:, m, :]

    def pass_up(k):
        block = up_all.at[behind(k), core]
        to_learner(UP, k, block, block).wait_recv()
        to_core(UP_CROSS, k, block, block).start()

    loop(1, n, pass_up)

    def got_up(k):
        block = up_all.at[behind(k), other]
        to_core(UP_CROSS, k, block, block).wait_recv()

    loop(1, n, got_up)

    for m in range(2):
        total = jnp.zeros((rank, tok.shape[0]), f32)
        for q in range(n):
            total = total + lax.dot_general(
                up_all[q, m], cot[m, :, q * kv_rows:(q + 1) * kv_rows],
                (((1,), (1,)), ((), ())), preferred_element_type=f32)
        total = total.astype(bf16)
        for q in range(n):
            back[q, m] = total[q * rows:(q + 1) * rows]

    locals_[3].wait()

    def grad_for(q):
        lhs = back[q].reshape(2 * rows, tok.shape[0])
        return adapter_scale * jnp.dot(lhs, tok[...], preferred_element_type=f32)

    def send_grad(k):
        q = ahead(k)
        g = grad_for(q).astype(bf16)
        grad_send[k, 0] = g[:rows]
        grad_send[k, 1] = g[rows:]
        to_learner(GRAD_DOWN, k, grad_send.at[k], grad_recv.at[k]).start()

    if relayed:
        relay_in = pltpu.make_async_remote_copy(
            src_ref=grad_send.at[0], dst_ref=grad_relay,
            send_sem=sems.at[RELAY, 0, 0], recv_sem=sems.at[RELAY, 1, 0],
            device_id={"dp": beside}, device_id_type=MESH,
        )

        @pl.when(middle)
        def _():
            send_grad(toward)
            send_grad(near)

        @pl.when(jnp.logical_not(middle))
        def _():
            g = grad_for(ahead(toward)).astype(bf16)
            grad_send[0, 0] = g[:rows]
            grad_send[0, 1] = g[rows:]
            relay_in.start()
            send_grad(2)
            send_grad(near)
    else:
        loop(1, n, send_grad)
    g = grad_for(me)
    grad_own[0] = g[:rows]
    grad_own[1] = g[rows:]
    locals_[6].wait()
    locals_[7].wait()
    for m in range(2):
        first[m] = first_raw[:, m, :]
        second[m] = second_raw[:, m, :]

    def low_for(q):
        part = lax.dot_general(
            down_all[q].reshape(2 * rows, tok.shape[1]), tok[...],
            (((1,), (1,)), ((), ())), preferred_element_type=f32)
        for m in range(2):
            low_own[m, q] = part[m * rows:(m + 1) * rows]
            low_send[m, q] = part[m * rows:(m + 1) * rows].astype(bf16)

    low_for(me)

    def take_down(k):
        q = behind(k)
        block = down_all.at[q]
        to_learner(DOWN, k, block, block).wait_recv()
        low_for(q)

    down_relay = None
    if relayed:
        take_down(2)
        block = down_all.at[behind(2)]
        down_relay = pltpu.make_async_remote_copy(
            src_ref=block, dst_ref=block,
            send_sem=sems.at[RELAY, 0, 1], recv_sem=sems.at[DOWN, 1, lax.rem(2 * me + 3, 4)],
            device_id={"dp": beside}, device_id_type=MESH,
        )

        @pl.when(middle)
        def _():
            down_relay.start()
            g = grad_for(ahead(2))
            relay_in.wait_recv()
            for m in range(2):
                grad_send[2, m] = (
                    g[m * rows:(m + 1) * rows] + grad_relay[m].astype(f32)).astype(bf16)
            to_learner(GRAD_DOWN, 2, grad_send.at[2], grad_recv.at[2]).start()

        take_down(toward)
        take_down(near)
    else:
        loop(1, n, take_down)
    half = to_core(LOW, 0, low_send.at[other], low_recv)
    half.start()
    half.wait()
    lowrank = (low_own[core] + low_recv[...].astype(f32)).astype(bf16).reshape(rank, tok.shape[0])

    gu = adapter_scale * jnp.dot(lowrank, cot[core], preferred_element_type=f32)
    for q in range(n):
        gu_own[q] = gu[:, q * kv_rows:(q + 1) * kv_rows]
        gu_send[q] = gu[:, q * kv_rows:(q + 1) * kv_rows].astype(bf16)

    loop(1, n, lambda k: to_learner(GRAD_UP, k, gu_send.at[ahead(k)], gu_recv.at[k]).start())
    gu_own[n] = gu_own[me]

    def add_up(k):
        to_learner(GRAD_UP, k, gu_send.at[ahead(k)], gu_recv.at[k]).wait_recv()
        gu_own[n] = gu_own[n] + gu_recv[k].astype(f32)

    loop(1, n, add_up)
    locals_[4].wait()
    locals_[5].wait()
    p, f, s = apply_adam_rule(up[core], up_first[core], up_second[core], gu_own[n])
    up_new_all[me, core] = p.astype(bf16)

    def send_new_up(k):
        block = up_new_all.at[me, core]
        to_learner(NEW_UP, k, block, block).start()

    loop(1, n, send_new_up)
    state[core, 0] = p
    state[core, 1] = f
    state[core, 2] = s
    mine = to_core(STATE, 0, state.at[core], state.at[core])
    mine.start()

    def got_grad(k):
        to_learner(GRAD_DOWN, k, grad_send.at[k], grad_recv.at[k]).wait_recv()

    if relayed:
        got_grad(2)
        got_grad(toward)
        pl.when(middle)(functools.partial(got_grad, near))
    else:
        loop(1, n, got_grad)

    def adam_down(k):
        q = ahead(k)
        cols = pl.ds(pl.multiple_of(q * width, 128), width)
        for m in range(2):
            g = grad_own[m, :, cols]
            for j in range(1, n):
                g = g + grad_recv[j, m, :, cols].astype(f32)
            p, f, s = apply_adam_rule(down[m, :, cols], first[m, :, cols], second[m, :, cols], g)
            down[m, :, cols] = p
            first[m, :, cols] = f
            second[m, :, cols] = s
            if isinstance(k, int) and k == 0:
                col_all[me, m] = p.astype(bf16)
            else:
                col_send[k, m] = p.astype(bf16)

    def send_columns(k):
        adam_down(k)
        to_learner(COLUMNS, k, col_send.at[k], col_all.at[me]).start()

    if relayed:
        send_columns(2)
        send_columns(toward)
        send_columns(near)
    else:
        loop(1, n, send_columns)
    adam_down(0)

    def pass_new_up(k):
        block = up_new_all.at[behind(k), core]
        to_learner(NEW_UP, k, block, block).wait_recv()
        to_core(NEW_UP_CROSS, k, block, block).start()

    loop(1, n, pass_new_up)
    outputs = []

    def write_out(src, dst):
        outputs.append(pltpu.make_async_copy(src, dst, out_sems.at[len(outputs)]))
        outputs[-1].start()

    to_core(STATE, 0, state.at[other], state.at[other]).wait_recv()
    for m in range(2):
        for i, out in enumerate((new_up, new_up_first, new_up_second)):
            write_out(state.at[m, i], out.at[m])
    up_new_all[me, other] = state[other, 0].astype(bf16)

    for new, raw, out in (
        (down, down_raw, new_down), (first, first_raw, new_first), (second, second_raw, new_second)
    ):
        for m in range(2):
            raw[:, m, :] = new[m]
        write_out(raw, out)

    def got_new_up(k):
        block = up_new_all.at[behind(k), other]
        to_core(NEW_UP_CROSS, k, block, block).wait_recv()

    loop(1, n, got_new_up)
    write_out(up_new_all, up_out)

    def got_columns(k):
        to_learner(COLUMNS, k, col_send.at[k], col_all.at[behind(k)]).wait_recv()

    loop(1, n, got_columns)
    write_out(col_all, columns_out)

    def sent(k):
        block = up_all.at[me, core]
        to_learner(UP, k, block, block).wait_send()
        block = up_all.at[behind(k), core]
        to_core(UP_CROSS, k, block, block).wait_send()
        to_learner(GRAD_UP, k, gu_send.at[ahead(k)], gu_recv.at[k]).wait_send()
        block = up_new_all.at[me, core]
        to_learner(NEW_UP, k, block, block).wait_send()
        block = up_new_all.at[behind(k), core]
        to_core(NEW_UP_CROSS, k, block, block).wait_send()
        to_learner(COLUMNS, k, col_send.at[k], col_all.at[me]).wait_send()

    def sent_down(k):
        block = down_all.at[me]
        to_learner(DOWN, k, block, block).wait_send()
        to_learner(GRAD_DOWN, k, grad_send.at[k], grad_recv.at[k]).wait_send()

    loop(1, n, sent)
    if relayed:
        sent_down(2)
        sent_down(near)

        @pl.when(middle)
        def _():
            sent_down(toward)
            down_relay.wait_send()

        @pl.when(jnp.logical_not(middle))
        def _():
            relay_in.wait_send()
    else:
        loop(1, n, sent_down)
    mine.wait_send()
    for c in outputs:
        c.wait()


def merge_kernel(
    frozen, up, columns, d0, d1, d2, u0, u1, u2,
    merged, e0, e1, e2, v0, v1, v2,
    start, result, up_in, cols_in, b0, b1, b2, b3, b4, b5, load_sems, store_sems, sems,
):
    n, _, rows, width = columns.shape
    rank, block = up.shape[2:]
    factors = [
        pltpu.make_async_copy(up, up_in, sems.at[2, 0]),
        pltpu.make_async_copy(columns, cols_in, sems.at[2, 1]),
    ]
    pieces = [(m, q) for m in range(2) for q in range(n)]
    loads, stores = [], []
    for m, q in pieces:
        part = pl.ds(q * block, block)
        loads.append(pltpu.make_async_copy(
            frozen.at[m, part], start.at[m, q], load_sems.at[m, q]))
        stores.append(pltpu.make_async_copy(
            result.at[m, q], merged.at[m, part], store_sems.at[m, q]))
    held = (b0, b1, b2, b3, b4, b5)
    ins = [
        pltpu.make_async_copy(a, b, sems.at[0, i])
        for i, (a, b) in enumerate(zip((d0, d1, d2, u0, u1, u2), held))
    ]
    outs = [
        pltpu.make_async_copy(b, a, sems.at[1, i])
        for i, (a, b) in enumerate(zip((e0, e1, e2, v0, v1, v2), held))
    ]
    for c in factors + loads[:2] + ins + loads[2:]:
        c.start()
    for c in factors:
        c.wait()
    for i, (m, q) in enumerate(pieces):
        change = lax.dot_general(
            adapter_scale * up_in[q, m], cols_in[:, m].reshape(n * rows, width),
            (((0,), (0,)), ((), ())), preferred_element_type=jnp.float32)
        loads[i].wait()
        result[m, q] = (start[m, q].astype(jnp.float32) + change).astype(result.dtype)
        stores[i].start()
        if i == 1:
            for c, e in zip(ins, outs):
                c.wait()
                e.start()
    for c in stores + outs:
        c.wait()


def local(
    n,
    tokens,
    cotangent,
    frozen_weight,
    adapter_down,
    down_first_moment,
    down_second_moment,
    adapter_up,
    up_first_moment,
    up_second_moment,
):
    bf16, f32 = jnp.bfloat16, jnp.float32
    tok, cot, frozen = tokens[0], cotangent[0], frozen_weight[0]
    down, first, second = adapter_down[0], down_first_moment[0], down_second_moment[0]
    up, up_first, up_second = [
        jnp.transpose(a[0], (1, 2, 0)) for a in (adapter_up, up_first_moment, up_second_moment)
    ]
    t, d = tok.shape
    _, kinds, o = cot.shape
    r = down.shape[0]
    rank, c = up.shape[1:]
    w = d // n
    hbm = pl.BlockSpec(memory_space=pltpu.HBM)
    down_like = jax.ShapeDtypeStruct(down.shape, f32)
    up_like = jax.ShapeDtypeStruct(up.shape, f32)
    outs = pl.pallas_call(
        functools.partial(exchange_kernel, n),
        out_shape=(
            down_like, down_like, down_like, up_like, up_like, up_like,
            jax.ShapeDtypeStruct((n, 2, r, w), bf16),
            jax.ShapeDtypeStruct((n, 2, rank, c), bf16),
        ),
        in_specs=[hbm] * 8,
        out_specs=(hbm,) * 8,
        scratch_shapes=[
            pltpu.VMEM((t, d), bf16),
            pltpu.VMEM((t, 2, o), bf16),
            pltpu.VMEM((2, t, o), bf16),
            pltpu.VMEM((r, 2, d), f32),
            pltpu.VMEM((r, 2, d), f32),
            pltpu.VMEM((r, 2, d), f32),
            pltpu.VMEM((2, r, d), f32),
            pltpu.VMEM((2, r, d), f32),
            pltpu.VMEM((2, r, d), f32),
            pltpu.VMEM((2, rank, c), f32),
            pltpu.VMEM((2, rank, c), f32),
            pltpu.VMEM((2, rank, c), f32),
            pltpu.VMEM((n, 2, rank, c), bf16),
            pltpu.VMEM((n, 2, r, d), bf16),
            pltpu.VMEM((n, 2, r, t), bf16),
            pltpu.VMEM((n, 2, r, d), bf16),
            pltpu.VMEM((n, 2, r, d), bf16),
            pltpu.VMEM((2, r, d), f32),
            pltpu.VMEM((2, n, r, t), f32),
            pltpu.VMEM((2, n, r, t), bf16),
            pltpu.VMEM((n, r, t), bf16),
            pltpu.VMEM((n, rank, c), bf16),
            pltpu.VMEM((n, rank, c), bf16),
            pltpu.VMEM((n + 1, rank, c), f32),
            pltpu.VMEM((n, 2, rank, c), bf16),
            pltpu.VMEM((2, 3, rank, c), f32),
            pltpu.VMEM((n, 2, r, w), bf16),
            pltpu.VMEM((n, 2, r, w), bf16),
            pltpu.VMEM((2, r, d), bf16),
            pltpu.SemaphoreType.DMA((KINDS, 2, n)),
            pltpu.SemaphoreType.DMA((8,)),
            pltpu.SemaphoreType.DMA((11,)),
        ],
        compiler_params=pltpu.CompilerParams(
            collective_id=0, has_side_effects=True, vmem_limit_bytes=60 * 1024 * 1024
        ),
        cost_estimate=pl.CostEstimate(flops=10**9, bytes_accessed=10**7, transcendentals=0),
    )(tok, cot, down, first, second, up, up_first, up_second)
    columns, up_cast = outs[6], outs[7]
    merged, *rest = pl.pallas_call(
        merge_kernel,
        out_shape=(
            jax.ShapeDtypeStruct((2, o, w), bf16),
            down_like, down_like, down_like, up_like, up_like, up_like,
        ),
        in_specs=[hbm] * 9,
        out_specs=(hbm,) * 7,
        scratch_shapes=[
            pltpu.VMEM((2, n, c, w), bf16),
            pltpu.VMEM((2, n, c, w), bf16),
            pltpu.VMEM((n, 2, rank, c), bf16),
            pltpu.VMEM((n, 2, r, w), bf16),
        ] + [pltpu.VMEM(down.shape, f32)] * 3 + [pltpu.VMEM(up.shape, f32)] * 3 + [
            pltpu.SemaphoreType.DMA((2, n)),
            pltpu.SemaphoreType.DMA((2, n)),
            pltpu.SemaphoreType.DMA((3, 6)),
        ],
        compiler_params=pltpu.CompilerParams(vmem_limit_bytes=60 * 1024 * 1024),
    )(frozen, up_cast, columns, *outs[:6])
    return (
        merged[None],
        rest[0][None],
        rest[1][None],
        rest[2][None],
        jnp.transpose(rest[3], (2, 0, 1))[None],
        jnp.transpose(rest[4], (2, 0, 1))[None],
        jnp.transpose(rest[5], (2, 0, 1))[None],
    )


def solution(mesh):
    return jax.shard_map(
        functools.partial(local, mesh.shape["dp"]),
        mesh=mesh,
        in_specs=(
            P("pipe", ("groups", "dp"), "sub"),
            P("pipe", ("groups", "dp"), None, None),
            P("pipe", None, None, ("sub", "dp")),
            P("pipe", "dp", "groups", "sub"),
            P("pipe", "dp", "groups", "sub"),
            P("pipe", "dp", "groups", "sub"),
            P("pipe", "dp", "groups", None),
            P("pipe", "dp", "groups", None),
            P("pipe", "dp", "groups", None),
        ),
        out_specs=(
            P("pipe", "groups", None, ("sub", "dp")),
            P("pipe", "dp", "groups", "sub"),
            P("pipe", "dp", "groups", "sub"),
            P("pipe", "dp", "groups", "sub"),
            P("pipe", "dp", "groups", None),
            P("pipe", "dp", "groups", None),
            P("pipe", "dp", "groups", None),
        ),
        check_vma=False,
    )
```
